512 devices in a mesh: ckpt: 8 (over x, z_hi), unit: 64 (over z_lo, y, core).
Axes of the slice: x: 4, y: 4, z: 16 (z_hi: 2, z_lo: 8; z = z_hi * 8 + z_lo), core: 2. Of those that a mesh axis runs over, the one named last changes fastest.
Arguments:
- train_acts: bfloat16 [8, 4096, 22016], P('ckpt', None, 'unit'), may hold values from -6 to 6
- train_grads: bfloat16 [8, 4096, 8192], P('ckpt', None, 'unit'), may hold values from -6 to 6
- query_acts: bfloat16 [8, 512, 22016], P('ckpt', None, 'unit'), may hold values from -6 to 6
- query_grads: bfloat16 [8, 512, 8192], P('ckpt', None, 'unit'), may hold values from -6 to 6
- query_segment: int32 [512], replicated, may hold values from 0 to 63, never falling along the last dimension, each value on 1 to 16 neighbouring positions
- proj_act: bfloat16 [22016, 64], P('unit'), may hold values from -0.0390625 to 0.0390625
- proj_grad: bfloat16 [8192, 64], P('unit'), may hold values from -0.0625 to 0.0625
- lrates: float32 [8], P('ckpt'), may hold values from 0.001 to 0.01
Outputs:
- scores: float32 [4096, 64], P('unit', 'ckpt')
The draws below stay inside these ranges and needn't reach their ends.
Inputs may be any that keep to these rules, and one draw needn't show every extreme that they name: `query_segment`: query tokens come grouped by sequence in order; each of the 64 sequences holds 1 to 16 tokens, one exactly 16.
All inputs are finite; a program needn't handle non-finite values.
Results may differ from the reference program's by a relative error of at most 0.0003.
Values may be sent and summed in bfloat16 or wider, within the bound.
A program may use at most 64 MiB of HBM per device.

```python
import math
import jax
import jax.numpy as jnp
import numpy as np
from jax import lax

D = 8192
FF = 22016
K1 = 64
K2 = 64
NQ = 64
QLEN = 16
QTOK = 512
TOKENS = 4096
NCK = 8


def block_levels(rng, shape, cuts, low, largest):
    def one(axis_at, blocks):
        heights = jax.random.uniform(jax.random.fold_in(jax.random.fold_in(rng, 6), axis_at), (blocks,), jnp.float32, low / len(cuts), largest / len(cuts))
        return jnp.repeat(jnp.exp(heights), shape[axis_at] // blocks).reshape((-1,) + (1,) * (len(shape) - axis_at - 1))

    factor_of = one(*cuts[0])
    for cut in cuts[1:]:
        factor_of = factor_of * one(*cut)
    return factor_of


def length_profile(count, total, reach, slope):
    portions = [(1 << 20) // math.isqrt(grade ** slope) + 1 for grade in range(2, count + 1)]
    spare, holding = total - reach - (count - 1), [1] * (count - 1)
    while spare > 0:
        candidates = [i for i in range(count - 1) if holding[i] < reach]
        pool, budget = sum([portions[i] for i in candidates]), spare
        for i in candidates:
            addition = min(reach - holding[i], max(1, budget * portions[i] // pool), spare)
            holding[i] = holding[i] + addition
            spare = spare - addition
    return np.array([reach] + holding)


def ragged(own_key, number_of, total, most, slope):
    if number_of == 2:
        one = jax.random.randint(own_key, (), max(1, total - most), min(most, total - 1) + 1)
        return jnp.stack([one, total - one])
    tallies = jnp.asarray(length_profile(number_of, total, most, slope), jnp.int32)
    pairs = (number_of - 1) // 2
    source_of, receiver = tallies[1:1 + 2 * pairs:2], tallies[2:2 + 2 * pairs:2]
    room = jnp.minimum(source_of - 1, most - receiver)
    passed = jax.random.randint(jax.random.fold_in(own_key, 1), (pairs,), 0, 1 << 20) % (room + 1)
    tallies = tallies.at[1:1 + 2 * pairs:2].set(source_of - passed).at[2:2 + 2 * pairs:2].set(receiver + passed)
    return tallies[jax.random.permutation(jax.random.fold_in(own_key, 2), number_of)]


def scatter_about(stream_key, shape, width, bound, shards=(), kind=jnp.bfloat16):
    result = width * jax.random.normal(stream_key, shape, jnp.float32)
    if shards:
        result = result * block_levels(stream_key, shape, shards, -0.22, 0.18)
    return jnp.clip(result, -bound, bound).astype(kind)


def setup_inputs(seed: int = 0) -> dict:
    key_of = jax.random.split(jax.random.key(seed), 9)
    return {
        "train_acts": scatter_about(key_of[0], (NCK, TOKENS, FF), 1.0, 6.0, ((0, 8), (2, 64))),
        "train_grads": scatter_about(key_of[1], (NCK, TOKENS, D), 1.0, 6.0, ((0, 8), (2, 64))),
        "query_acts": scatter_about(key_of[2], (NCK, QTOK, FF), 1.0, 6.0, ((0, 8), (2, 64))),
        "query_grads": scatter_about(key_of[3], (NCK, QTOK, D), 1.0, 6.0, ((0, 8), (2, 64))),
        "query_segment": jnp.searchsorted(jnp.cumsum(ragged(key_of[4], NQ, QTOK, QLEN, 0)), jnp.arange(QTOK), side="right").astype(jnp.int32),
        "proj_act": scatter_about(key_of[5], (FF, K1), FF ** -0.5, 0.0390625, ((0, 64),)),
        "proj_grad": scatter_about(key_of[6], (D, K2), D ** -0.5, 0.0625, ((0, 64),)),
        "lrates": jnp.clip(jnp.exp(math.log(0.01) - 2.30258502 * jax.random.uniform(key_of[7], (NCK,), jnp.float32) ** block_levels(key_of[7], (NCK,), ((0, 8),), -0.2, 0.2)), 0.001, 0.01),
    }


def reference(train_acts, train_grads, query_acts, query_grads, query_segment, proj_act, proj_grad, lrates):
    highest = lax.Precision.HIGHEST
    onehot = (query_segment[:, None] == jnp.arange(NQ, dtype=jnp.int32)[None, :]).astype(jnp.float32)
    basis_act = proj_act.astype(jnp.float32)
    basis_grad = proj_grad.astype(jnp.float32)
    summed = jnp.zeros((TOKENS, NQ), jnp.float32)
    for ckpt_id in range(NCK):
        train_a = jnp.dot(train_acts[ckpt_id].astype(jnp.float32), basis_act, precision=highest)
        train_g = jnp.dot(train_grads[ckpt_id].astype(jnp.float32), basis_grad, precision=highest)
        query_a = jnp.dot(query_acts[ckpt_id].astype(jnp.float32), basis_act, precision=highest)
        query_g = jnp.dot(query_grads[ckpt_id].astype(jnp.float32), basis_grad, precision=highest)
        query_outer = jnp.einsum('sq,si,sj->qij', onehot, query_a, query_g, precision=highest)
        middle = jnp.einsum('ti,qij->tqj', train_a, query_outer, precision=highest)
        ckpt_score = jnp.sum(middle * train_g[:, None, :], axis=2)
        summed = summed + lrates[ckpt_id] * ckpt_score
    return summed
```

```python
import jax
import jax.numpy as jnp
from jax import lax
from jax.experimental import pallas as pl
from jax.experimental.pallas import tpu as pltpu
from jax.sharding import PartitionSpec as P

MESH = pl.DeviceIdType.MESH
NX, NZ, NY = 4, 8, 4
NQ = 64
ROWS = 64
BLOCK = NY * 2 * ROWS
HALF = 64
QTOK = 512
LANES = 128


def flip(v, bit):
    return v + bit - 2 * bit * lax.rem(lax.div(v, bit), 2)


def kernel(
    ta, tg, qa, qg, seg, pa, pg, lr, out,
    xa, xg, xqa, xqg, xseg, wa, wg, xlr, ins,
    part, c_in, y1_out, y1_in, y2_out, y2_in, acc, z_in,
    qpart, qc_in, qy_out, qy_in, qz_out, qz_in, qall, p_out, p_in, s_out, s_in,
    ssem, rsem,
):
    c = lax.axis_index("ckpt")
    u = lax.axis_index("unit")
    x, zh = lax.div(c, 2), lax.rem(c, 2)
    z, y, k = lax.div(u, 8), lax.rem(lax.div(u, 2), 4), lax.rem(u, 2)

    def at(x_, zh_, z_, y_, k_):
        return (x_ * 2 + zh_, (z_ * NY + y_) * 2 + k_)

    def p1(v):
        return (1 - k) * flip(v, 1) + k * (3 - v)

    def p2(v):
        return (1 - k) * (3 - v) + k * flip(v, 1)

    ya, yb = p1(y), p2(y)
    sib = at(x, zh, z, y, 1 - k)
    y_peers = [at(x, zh, z, lax.rem(y + d, NY), k) for d in range(1, NY)]
    z_peers = [at(x, zh, lax.rem(z + d, NZ), y, k) for d in range(1, NZ)]
    home = flip(z, 4)
    c_peers = [
        at(lax.rem(x + d, NX), lax.rem(zh + e, 2), home, y, k)
        for d in range(NX)
        for e in range(2)
    ]
    partners = [sib] + y_peers + z_peers + c_peers[1:]

    loads = {}

    def load(name, src, dst):
        cp = pltpu.make_async_copy(src, dst, ins.at[len(loads)])
        cp.start()
        loads[name] = cp

    load("qa", qa, xqa)
    load("qg", qg, xqg)
    load("pa", pa, wa)
    load("pg", pg, wg)

    def by_bits(m):
        v = z
        for b in (1, 2, 4):
            if m & b:
                v = flip(v, b)
        return v

    for m in range(NZ - 1, -1, -1):
        cols = pl.ds(pl.multiple_of(by_bits(m ^ 4) * BLOCK, BLOCK), BLOCK)
        load(f"ta{m}", ta.at[:, cols], xa.at[m])
        load(f"tg{m}", tg.at[cols], xg.at[m])
    load("seg", seg, xseg)
    load("lr", lr, xlr)

    barrier = pltpu.get_barrier_semaphore()
    for p in partners:
        pl.semaphore_signal(barrier, inc=1, device_id=p, device_id_type=MESH)

    sent = []

    def send(src, dst, to):
        i = len(sent)
        cp = pltpu.make_async_remote_copy(
            src_ref=src, dst_ref=dst, send_sem=ssem.at[i], recv_sem=rsem.at[i],
            device_id=to, device_id_type=MESH,
        )
        cp.start()
        sent.append(cp)
        return cp

    def project(dst, acts, grads):
        a = jnp.dot(wa[...], acts, preferred_element_type=jnp.float32)
        g = lax.dot_general(
            wg[...], grads, (((1,), (1,)), ((), ())), preferred_element_type=jnp.float32
        )
        for j in range(NY):
            dst[0, j] = a[:, j * LANES : (j + 1) * LANES]
            dst[1, j] = g[:, j * LANES : (j + 1) * LANES]

    for n in ("pa", "pg", "qa", "qg"):
        loads[n].wait()
    project(qpart, xqa[...], xqg[...])
    pl.semaphore_wait(barrier, len(partners))
    qc = send(qpart.at[1 - k], qc_in, sib)

    c_cp, y1_cp, y2_cp, z_cp = {}, {}, {}, {}

    def stage_c(m):
        loads[f"ta{m}"].wait()
        loads[f"tg{m}"].wait()
        project(part.at[m], xa[m], xg[m])
        c_cp[m] = send(part.at[m, 1 - k], c_in.at[m], sib)

    def stage_y1(m):
        c_cp[m].wait_recv()
        y1_out[m, 0] = part[m, k, ya] + c_in[m, ya]
        yab = p2(ya)
        y1_out[m, 1] = part[m, k, yab] + c_in[m, yab]
        y1_cp[m] = send(y1_out.at[m], y1_in.at[m], at(x, zh, z, ya, k))

    def stage_y2(m):
        y1_cp[m].wait_recv()
        y2_out[m] = part[m, k, yb] + c_in[m, yb] + y1_in[m, 1]
        y2_cp[m] = send(y2_out.at[m], y2_in.at[m], at(x, zh, z, yb, k))
        acc[m] = part[m, k, y] + c_in[m, y] + y1_in[m, 0]

    def stage_z1(m):
        y2_cp[m].wait_recv()
        acc[m] = acc[m] + y2_in[m]
        if m & 1:
            z_cp[m] = send(acc.at[m], z_in.at[m], at(x, zh, flip(z, 1), y, k))

    def stage_z2(m):
        z_cp[m + 1].wait_recv()
        acc[m] = acc[m] + z_in[m + 1]
        if m & 2:
            z_cp[m] = send(acc.at[m], z_in.at[m], at(x, zh, flip(z, 2), y, k))

    def stage_z3(m):
        z_cp[m + 2].wait_recv()
        acc[m] = acc[m] + z_in[m + 2]
        if m & 4:
            z_cp[m] = send(acc.at[m], z_in.at[m], at(x, zh, flip(z, 4), y, k))

    stage_c(7)
    stage_c(6)
    qc.wait_recv()
    for j in range(NY):
        qy_out[j] = qpart[k, j] + qc_in[j]
    qy = []
    for d in range(1, NY):
        qy.append(send(qy_out.at[lax.rem(y + d, NY)], qy_in.at[d - 1], y_peers[d - 1]))
    stage_c(5)
    stage_c(4)
    stage_y1(7)
    stage_y1(6)
    stage_c(3)
    stage_c(2)
    for cp in qy:
        cp.wait_recv()
    qz_out[...] = (qy_out[y] + qy_in[0] + qy_in[1] + qy_in[2]).reshape(qz_out.shape)
    qz = []
    for d in range(1, NZ):
        qz.append(send(qz_out.at[lax.rem(z + d, NZ)], qz_in.at[d - 1], z_peers[d - 1]))
    stage_y1(5)
    stage_y1(4)
    stage_c(1)
    stage_c(0)
    stage_y1(3)
    stage_y1(2)
    stage_y2(7)
    stage_y2(6)
    stage_y1(1)
    stage_y1(0)
    stage_y2(5)
    stage_y2(4)
    stage_z1(7)
    stage_z1(6)
    for cp in qz:
        cp.wait_recv()
    total = qz_out[z]
    for d in range(NZ - 1):
        total = total + qz_in[d]
    qall[y, z] = total
    mine = qall.at[y, z]
    qz = [send(mine, mine, p) for p in z_peers]
    stage_y2(3)
    stage_y2(2)
    stage_z1(5)
    stage_z1(4)
    stage_z2(6)
    stage_y2(1)
    stage_y2(0)
    stage_z2(4)
    stage_z1(3)
    stage_z1(2)
    stage_z3(4)
    stage_z1(1)
    stage_z1(0)
    stage_z2(2)
    for cp in qz:
        cp.wait_recv()
    line = qall.at[y]
    qy = [send(line, line, p) for p in y_peers]
    stage_z2(0)
    stage_z3(0)
    loads["seg"].wait()
    loads["lr"].wait()
    onehot = (
        lax.broadcasted_iota(jnp.int32, (NQ, QTOK), 0) == xseg[...]
    ).astype(jnp.float32)
    z_cp[4].wait_recv()
    tok = (acc[0] + z_in[4]).T
    for cp in qy:
        cp.wait_recv()
    for j in range(NY):
        match = jnp.dot(
            tok, qall[j].reshape(HALF, LANES),
            precision=lax.Precision.HIGHEST, preferred_element_type=jnp.float32,
        )
        p_out[:, j] = match.reshape(2, ROWS, LANES)
    pc = send(p_out.at[1 - k], p_in, sib)
    pc.wait_recv()
    score = jnp.zeros((NQ, LANES), jnp.float32)
    for j in range(NY):
        prod = p_out[k, j] * p_in[j]
        score += lax.dot_general(
            onehot[:, j * LANES : (j + 1) * LANES],
            jnp.concatenate([prod, prod], axis=0),
            (((1,), (1,)), ((), ())),
            precision=lax.Precision.HIGHEST, preferred_element_type=jnp.float32,
        )
    s_out[...] = (xlr[0] * score).reshape(s_out.shape)
    fin = []
    for i, p in enumerate(c_peers):
        fin.append(send(s_out.at[p[0]], s_in.at[i], p))
    for cp in fin:
        cp.wait_recv()
    total = s_in[0]
    for i in range(1, len(c_peers)):
        total = total + s_in[i]
    out[...] = total[:, :ROWS]
    for cp in sent:
        cp.wait_send()


def body(
    train_acts, train_grads, query_acts, query_grads, query_segment, proj_act, proj_grad, lrates
):
    ff, d = train_acts.shape[2], train_grads.shape[2]
    f32, bf16 = jnp.float32, jnp.bfloat16
    vmem = pltpu.VMEM
    nsend = 80
    hbm = pl.BlockSpec(memory_space=pltpu.HBM)
    res = pl.pallas_call(
        kernel,
        out_shape=jax.ShapeDtypeStruct((8, ROWS), f32),
        in_specs=[hbm] * 8,
        out_specs=pl.BlockSpec(memory_space=pltpu.VMEM),
        scratch_shapes=[
            vmem((NZ, ff, BLOCK), bf16),
            vmem((NZ, BLOCK, d), bf16),
            vmem((ff, QTOK), bf16),
            vmem((QTOK, d), bf16),
            vmem((1, QTOK), jnp.int32),
            vmem((HALF, ff), bf16),
            vmem((HALF, d), bf16),
            pltpu.SMEM((1,), f32),
            pltpu.SemaphoreType.DMA((2 * NZ + 6,)),
            vmem((NZ, 2, NY, HALF, LANES), f32),
            vmem((NZ, NY, HALF, LANES), f32),
            vmem((NZ, 2, HALF, LANES), f32),
            vmem((NZ, 2, HALF, LANES), f32),
            vmem((NZ, HALF, LANES), f32),
            vmem((NZ, HALF, LANES), f32),
            vmem((NZ, HALF, LANES), f32),
            vmem((NZ, HALF, LANES), f32),
            vmem((2, NY, HALF, LANES), f32),
            vmem((NY, HALF, LANES), f32),
            vmem((NY, HALF, LANES), f32),
            vmem((NY - 1, HALF, LANES), f32),
            vmem((NZ, 8, LANES), f32),
            vmem((NZ - 1, 8, LANES), f32),
            vmem((NY, NZ, 8, LANES), f32),
            vmem((2, NY, ROWS, LANES), f32),
            vmem((NY, ROWS, LANES), f32),
            vmem((8, 8, LANES), f32),
            vmem((8, 8, LANES), f32),
            pltpu.SemaphoreType.DMA((nsend,)),
            pltpu.SemaphoreType.DMA((nsend,)),
        ],
        compiler_params=pltpu.CompilerParams(
            collective_id=0, has_side_effects=True, vmem_limit_bytes=60 << 20
        ),
        name="tracin",
    )(
        train_acts[0].T,
        train_grads[0],
        query_acts[0].T,
        query_grads[0],
        query_segment.reshape(1, QTOK),
        proj_act.T,
        proj_grad.T,
        lrates,
    )
    return res.T


def solution(mesh):
    placed = (
        P("ckpt", None, "unit"),
        P("ckpt", None, "unit"),
        P("ckpt", None, "unit"),
        P("ckpt", None, "unit"),
        P(),
        P("unit", None),
        P("unit", None),
        P("ckpt"),
    )
    return jax.shard_map(
        body, mesh=mesh, in_specs=placed, out_specs=P("unit", "ckpt"), check_vma=False
    )
```

```python
import jax
import jax.numpy as jnp
from jax import lax
from jax.experimental import pallas as pl
from jax.experimental.pallas import tpu as pltpu
from jax.sharding import PartitionSpec as P

MESH = pl.DeviceIdType.MESH
NX, NZ, NY = 4, 8, 4
NQ = 64
ROWS = 64
BLOCK = NY * 2 * ROWS
NP = NZ // 2
HALF = 64
QH = HALF // 2
SCALE = 16
QTOK = 512
LANES = 128
TOP = 32760.0


def flip(v, bit):
    return v + bit - 2 * bit * lax.rem(lax.div(v, bit), 2)


def put(ref, groups):
    at, logs = 0, []
    for blocks in groups:
        top = jnp.max(jnp.abs(blocks[0]), axis=0, keepdims=True)
        for v in blocks[1:]:
            top = jnp.maximum(top, jnp.max(jnp.abs(v), axis=0, keepdims=True))
        log = jnp.ceil(jnp.log2(jnp.maximum(top, 1e-30)) * 256.0)
        unit = jnp.exp2(log * (-1.0 / 256.0)) * TOP
        for v in blocks:
            n = v.shape[0]
            ref[at : at + n] = jnp.round(v * unit).astype(jnp.int32).astype(jnp.int16)
            at += n
        logs.append(jnp.broadcast_to(log.astype(jnp.int32), (SCALE // len(groups), LANES)))
    ref[at : at + SCALE] = jnp.concatenate(logs, axis=0).astype(jnp.int16)


def get(ref, groups, rows):
    n = ref.shape[0] - SCALE
    logs = ref[n:].astype(jnp.int32).astype(jnp.float32)
    step = SCALE // groups
    found = []
    for i in range(groups):
        unit = jnp.exp2(logs[i * step : i * step + 1] * (1.0 / 256.0)) * (1.0 / TOP)
        start, end = i * n // groups, (i + 1) * n // groups
        found.append([
            ref[r : r + rows].astype(jnp.int32).astype(jnp.float32) * unit
            for r in range(start, end, rows)
        ])
    return found


def kernel(
    ta, tg, qa, qg, seg, pa, pg, lr, out,
    xa, xg, xqa, xqg, xseg, wa, wg, xlr, ins,
    part, c_in, y1_out, y1_in, y2_out, y2_in, z_out, z_in, keep, acc,
    qpart, qc_in, qy_own, qy_out, qy_in, qz_own, qz_out, qz_in, qall, p_out, p_in, s_out, s_in,
    ssem, rsem,
):
    c = lax.axis_index("ckpt")
    u = lax.axis_index("unit")
    x, zh = lax.div(c, 2), lax.rem(c, 2)
    z, y, k = lax.div(u, 8), lax.rem(lax.div(u, 2), 4), lax.rem(u, 2)

    def at(x_, zh_, z_, y_, k_):
        return (x_ * 2 + zh_, (z_ * NY + y_) * 2 + k_)

    def p1(v):
        return (1 - k) * flip(v, 1) + k * (3 - v)

    def p2(v):
        return (1 - k) * (3 - v) + k * flip(v, 1)

    ya, yb = p1(y), p2(y)
    yab = p2(ya)
    sib = at(x, zh, z, y, 1 - k)
    y_peers = [at(x, zh, z, lax.rem(y + d, NY), k) for d in range(1, NY)]
    z_peers = [at(x, zh, lax.rem(z + d, NZ), y, k) for d in range(1, NZ)]
    home = flip(z, 4)
    c_peers = [
        at(lax.rem(x + d, NX), lax.rem(zh + e, 2), home, y, k)
        for d in range(NX)
        for e in range(2)
    ]
    partners = [sib] + y_peers + z_peers + c_peers[1:]

    barrier = pltpu.get_barrier_semaphore()
    for p in partners:
        pl.semaphore_signal(barrier, inc=1, device_id=p, device_id_type=MESH)

    loads = {}

    def load(name, src, dst):
        cp = pltpu.make_async_copy(src, dst, ins.at[len(loads)])
        cp.start()
        loads[name] = cp

    load("qa", qa, xqa)
    load("qg", qg, xqg)
    load("pa", pa, wa)
    load("pg", pg, wg)
    zp = lax.div(z, 2)
    for w in range(NP - 1, -1, -1):
        b = flip(zp, 2)
        for bit in (1, 2):
            b = flip(b, bit) if w & bit else b
        cols = pl.ds(pl.multiple_of(b * (2 * BLOCK), 2 * BLOCK), 2 * BLOCK)
        load(f"ta{w}", ta.at[:, cols], xa.at[w])
        load(f"tg{w}", tg.at[cols], xg.at[w])
    load("seg", seg, xseg)
    load("lr", lr, xlr)

    sems = [0]
    sent = []

    def copy_to(src, dst, to, i):
        return pltpu.make_async_remote_copy(
            src_ref=src, dst_ref=dst, send_sem=ssem.at[i], recv_sem=rsem.at[i],
            device_id=to, device_id_type=MESH,
        )

    def send(src, dst, to):
        cp = copy_to(src, dst, to, sems[0])
        sems[0] += 1
        cp.start()
        sent.append(cp)
        return cp

    def project(acts, grads, store):
        a = jnp.dot(wa[...], acts, preferred_element_type=jnp.float32)
        g = lax.dot_general(
            wg[...], grads, (((1,), (1,)), ((), ())), preferred_element_type=jnp.float32
        )
        for j in range(a.shape[1] // LANES):
            store(0, j, a[:, j * LANES : (j + 1) * LANES])
            store(1, j, g[:, j * LANES : (j + 1) * LANES])

    def project_query():
        for n in ("pa", "pg", "qa", "qg"):
            loads[n].wait()

        def store(h, j, v):
            qpart[h, j] = v

        project(xqa[...], xqg[...], store)

    def project_pair(w):
        loads[f"ta{w}"].wait()
        loads[f"tg{w}"].wait()

        def store(h, j, v):
            part[w, h, j // NY, j % NY] = v

        project(xa[w], xg[w], store)

    cp = {}

    def send_c(w):
        cp["c", w] = send(part.at[w, 1 - k], c_in.at[w], sib)

    def own(w, i, v):
        return part[w, k, i, v] + c_in[w, i, v]

    def stage_y1(w):
        cp["c", w].wait_recv()
        put(y1_out.at[w], [[own(w, i, ya), own(w, i, yab)] for i in range(2)])
        cp["y1", w] = send(y1_out.at[w], y1_in.at[w], at(x, zh, z, ya, k))

    def stage_y2(w):
        cp["y1", w].wait_recv()
        got = get(y1_in.at[w], 2, HALF)
        put(y2_out.at[w], [[own(w, i, yb) + got[i][1]] for i in range(2)])
        cp["y2", w] = send(y2_out.at[w], y2_in.at[w], at(x, zh, z, yb, k))
        for i in range(2):
            keep[w, i] = own(w, i, y) + got[i][0]

    def stage_z1(w):
        cp["y2", w].wait_recv()
        got = get(y2_in.at[w], 2, HALF)
        for i in range(2):
            keep[w, i] = keep[w, i] + got[i][0]
        mine = lax.rem(z, 2)
        put(z_out.at[w, 0], [[keep[w, 1 - mine]]])
        cp["z1", w] = send(z_out.at[w, 0], z_in.at[w, 0], at(x, zh, flip(z, 1), y, k))
        acc[w] = keep[w, mine]

    def stage_z2(w):
        cp["z1", w].wait_recv()
        v = acc[w] + get(z_in.at[w, 0], 1, HALF)[0][0]
        if w % 2:
            put(z_out.at[w, 1], [[v]])
            cp["z2", w] = send(z_out.at[w, 1], z_in.at[w, 1], at(x, zh, flip(z, 2), y, k))
        else:
            acc[w] = v

    def stage_z3():
        cp["z2", 3].wait_recv()
        put(z_out.at[2, 1], [[acc[2] + get(z_in.at[3, 1], 1, HALF)[0][0]]])
        cp["z3"] = send(z_out.at[2, 1], z_in.at[2, 1], at(x, zh, flip(z, 4), y, k))

    project_query()
    project_pair(3)
    pl.semaphore_wait(barrier, len(partners))
    qc = send(qpart.at[1 - k], qc_in, sib)
    send_c(3)
    project_pair(2)
    send_c(2)
    qc.wait_recv()
    for j in range(NY):
        v = qpart[k, j] + qc_in[j]
        qy_own[j] = v
        put(qy_out.at[j], [[v]])
    qy = [
        send(qy_out.at[lax.rem(y + d, NY)], qy_in.at[d - 1], y_peers[d - 1])
        for d in range(1, NY)
    ]
    stage_y1(3)
    project_pair(1)
    send_c(1)
    stage_y1(2)
    project_pair(0)
    send_c(0)
    stage_y1(1)
    stage_y1(0)
    for p in qy:
        p.wait_recv()
    v = qy_own[y]
    for d in range(NY - 1):
        v = v + get(qy_in.at[d], 1, HALF)[0][0]
    first_z, first_b = sems[0], sems[0] + NZ
    sems[0] += 2 * NZ + 2
    middle = (NZ // 2 - 1, NZ // 2)
    for h in range(2):
        qz_own[h] = v[h * QH : (h + 1) * QH]
        put(qz_out.at[h], [[v[h * QH : (h + 1) * QH]]])

    def to_middle(h):
        d = lax.rem(z - middle[h] + NZ, NZ)
        return pltpu.make_async_remote_copy(
            src_ref=qz_out.at[h], dst_ref=qz_in.at[d], send_sem=ssem.at[first_z + h],
            recv_sem=rsem.at[first_z + d], device_id=at(x, zh, middle[h], y, k),
            device_id_type=MESH,
        )

    for h in range(2):

        @pl.when(z != middle[h])
        def _():
            to_middle(h).start()

    is_middle = jnp.logical_or(z == middle[0], z == middle[1])
    my_h = 1 - lax.rem(z, 2)

    def from_middle(d):
        place = qall.at[y, my_h]
        return pltpu.make_async_remote_copy(
            src_ref=place, dst_ref=place, send_sem=ssem.at[first_b + 1 + d],
            recv_sem=rsem.at[first_b + my_h], device_id=z_peers[d - 1], device_id_type=MESH,
        )

    def middle_sum():
        @pl.when(is_middle)
        def _():
            total = qz_own[my_h]
            for d in range(1, NZ):
                copy_to(qz_out.at[0], qz_in.at[d], sib, first_z + d).wait_recv()
            for d in range(1, NZ):
                total = total + get(qz_in.at[d], 1, QH)[0][0]
            put(qall.at[y, my_h], [[total]])
            for d in range(1, NZ):
                from_middle(d).start()

    stage_y2(3)
    stage_y2(2)
    stage_y2(1)
    stage_y2(0)
    stage_z1(3)
    stage_z1(2)
    middle_sum()
    stage_z2(3)
    stage_z1(1)
    stage_z2(2)
    stage_z1(0)
    stage_z3()
    stage_z2(1)
    stage_z2(0)
    loads["seg"].wait()
    loads["lr"].wait()
    onehot = jnp.where(
        lax.broadcasted_iota(jnp.int32, (NQ, QTOK), 0) == xseg[...], 1.0, 0.0
    ).astype(jnp.bfloat16)
    for h in range(2):

        @pl.when(z != middle[h])
        def _():
            copy_to(qall.at[y, h], qall.at[y, h], sib, first_b + h).wait_recv()

    line = qall.at[y]
    qy = [send(line, line, p) for p in y_peers]
    cp["z2", 1].wait_recv()
    v = acc[0] + get(z_in.at[1, 1], 1, HALF)[0][0]
    cp["z3"].wait_recv()
    tok = (v + get(z_in.at[2, 1], 1, HALF)[0][0]).T
    for p in qy:
        p.wait_recv()
    for j in range(NY):
        feats = jnp.concatenate([get(qall.at[j, h], 1, QH)[0][0] for h in range(2)], axis=0)
        match = jnp.dot(
            tok, feats, precision=lax.Precision.HIGHEST, preferred_element_type=jnp.float32
        )
        p_out[:, j] = match.reshape(2, ROWS, LANES)
    pc = send(p_out.at[1 - k], p_in, sib)
    pc.wait_recv()
    score = jnp.zeros((NQ, LANES), jnp.float32)
    for j in range(NY):
        prod = p_out[k, j] * p_in[j]
        high = prod.astype(jnp.bfloat16)
        rest = (prod - high.astype(jnp.float32)).astype(jnp.bfloat16)
        score += lax.dot_general(
            onehot[:, j * LANES : (j + 1) * LANES],
            jnp.concatenate([high, rest], axis=0),
            (((1,), (1,)), ((), ())), preferred_element_type=jnp.float32,
        )
    score = xlr[0] * (score + pltpu.roll(score, ROWS, 1))
    s_out[...] = score.reshape(s_out.shape)
    fin = []
    for i, p in enumerate(c_peers):
        fin.append(send(s_out.at[p[0]], s_in.at[i], p))
    for p in fin:
        p.wait_recv()
    total = s_in[0]
    for i in range(1, len(c_peers)):
        total = total + s_in[i]
    out[...] = total[:, :ROWS]
    for p in sent:
        p.wait_send()
    for h in range(2):

        @pl.when(z != middle[h])
        def _():
            to_middle(h).wait_send()

    @pl.when(is_middle)
    def _():
        for d in range(1, NZ):
            from_middle(d).wait_send()


def body(
    train_acts, train_grads, query_acts, query_grads, query_segment, proj_act, proj_grad, lrates
):
    ff, d = train_acts.shape[2], train_grads.shape[2]
    f32, bf16, i16 = jnp.float32, jnp.bfloat16, jnp.int16
    vmem = pltpu.VMEM
    nsem = 80
    hbm = pl.BlockSpec(memory_space=pltpu.HBM)
    res = pl.pallas_call(
        kernel,
        out_shape=jax.ShapeDtypeStruct((8, ROWS), f32),
        in_specs=[hbm] * 8,
        out_specs=pl.BlockSpec(memory_space=pltpu.VMEM),
        scratch_shapes=[
            vmem((NP, ff, 2 * BLOCK), bf16),
            vmem((NP, 2 * BLOCK, d), bf16),
            vmem((ff, QTOK), bf16),
            vmem((QTOK, d), bf16),
            vmem((1, QTOK), jnp.int32),
            vmem((HALF, ff), bf16),
            vmem((HALF, d), bf16),
            pltpu.SMEM((1,), f32),
            pltpu.SemaphoreType.DMA((2 * NP + 6,)),
            vmem((NP, 2, 2, NY, HALF, LANES), f32),
            vmem((NP, 2, NY, HALF, LANES), f32),
            vmem((NP, 4 * HALF + SCALE, LANES), i16),
            vmem((NP, 4 * HALF + SCALE, LANES), i16),
            vmem((NP, 2 * HALF + SCALE, LANES), i16),
            vmem((NP, 2 * HALF + SCALE, LANES), i16),
            vmem((NP, 2, HALF + SCALE, LANES), i16),
            vmem((NP, 2, HALF + SCALE, LANES), i16),
            vmem((NP, 2, HALF, LANES), f32),
            vmem((NP, HALF, LANES), f32),
            vmem((2, NY, HALF, LANES), f32),
            vmem((NY, HALF, LANES), f32),
            vmem((NY, HALF, LANES), f32),
            vmem((NY, HALF + SCALE, LANES), i16),
            vmem((NY - 1, HALF + SCALE, LANES), i16),
            vmem((2, QH, LANES), f32),
            vmem((2, QH + SCALE, LANES), i16),
            vmem((NZ, QH + SCALE, LANES), i16),
            vmem((NY, 2, QH + SCALE, LANES), i16),
            vmem((2, NY, ROWS, LANES), f32),
            vmem((NY, ROWS, LANES), f32),
            vmem((8, 8, LANES), f32),
            vmem((8, 8, LANES), f32),
            pltpu.SemaphoreType.DMA((nsem,)),
            pltpu.SemaphoreType.DMA((nsem,)),
        ],
        compiler_params=pltpu.CompilerParams(
            collective_id=0, has_side_effects=True, vmem_limit_bytes=60 << 20
        ),
        name="tracin",
    )(
        train_acts[0].T,
        train_grads[0],
        query_acts[0].T,
        query_grads[0],
        query_segment.reshape(1, QTOK),
        proj_act.T,
        proj_grad.T,
        lrates,
    )
    return res.T


def solution(mesh):
    placed = (
        P("ckpt", None, "unit"),
        P("ckpt", None, "unit"),
        P("ckpt", None, "unit"),
        P("ckpt", None, "unit"),
        P(),
        P("unit", None),
        P("unit", None),
        P("ckpt"),
    )
    return jax.shard_map(
        body, mesh=mesh, in_specs=placed, out_specs=P("unit", "ckpt"), check_vma=False
    )
```

```python
import jax
import jax.numpy as jnp
from jax import lax
from jax.experimental import pallas as pl
from jax.experimental.pallas import tpu as pltpu
from jax.sharding import PartitionSpec as P

MESH = pl.DeviceIdType.MESH
NX, NZ, NY = 4, 8, 4
NQ = 64
ROWS = 64
BLOCK = NY * 2 * ROWS
NP = NZ // 2
HALF = 64
QH = HALF // 2
QTOK = 512
LANES = 128
TOP = 32760.0


def flip(v, bit):
    return v + bit - 2 * bit * lax.rem(lax.div(v, bit), 2)


def put(ref, groups):
    at, logs = 0, []
    for blocks in groups:
        top = jnp.max(jnp.abs(blocks[0]), axis=0, keepdims=True)
        for v in blocks[1:]:
            top = jnp.maximum(top, jnp.max(jnp.abs(v), axis=0, keepdims=True))
        log = jnp.ceil(jnp.log2(jnp.maximum(top, 1e-30)) * 256.0)
        unit = jnp.exp2(log * (-1.0 / 256.0)) * TOP
        for v in blocks:
            q = jnp.round(v * unit).astype(jnp.int32)
            n = v.shape[0] // 2
            ref[at : at + n] = (q[n:] << 16) | (q[:n] & 0xFFFF)
            at += n
        logs.append(log.astype(jnp.int32))
    for log in logs:
        ref[at : at + 1] = log
        at += 1


def get(ref, groups, rows):
    n, half = ref.shape[0] - groups, rows // 2
    found = []
    for i in range(groups):
        log = ref[n + i : n + i + 1].astype(jnp.float32)
        unit = jnp.exp2(log * (1.0 / 256.0)) * (1.0 / TOP)
        blocks = []
        for r in range(i * n // groups, (i + 1) * n // groups, half):
            v = ref[r : r + half]
            both = jnp.concatenate([(v << 16) >> 16, v >> 16], axis=0)
            blocks.append(both.astype(jnp.float32) * unit)
        found.append(blocks)
    return found


def kernel(
    ta, tg, qa, qg, seg, pa, pg, lr, out,
    xa, xg, xqa, xqg, xseg, wa, wg, xlr, ins,
    part, c_in, y1_out, y1_in, y2_out, y2_in, z_out, z_in, f_out, f_in, keep,
    qpart, qc_in, qy_own, qy_out, qy_in, qz_own, qz_out, qz_in, qall, p_out, p_in, s_out, s_in,
    ssem, rsem, z_sem, x_sem,
):
    c = lax.axis_index("ckpt")
    u = lax.axis_index("unit")
    x, zh = lax.div(c, 2), lax.rem(c, 2)
    z, y, k = lax.div(u, 8), lax.rem(lax.div(u, 2), 4), lax.rem(u, 2)

    def at(x_, zh_, z_, y_, k_):
        return (x_ * 2 + zh_, (z_ * NY + y_) * 2 + k_)

    def p1(v):
        return k * flip(v, 1) + (1 - k) * (3 - v)

    def p2(v):
        return k * (3 - v) + (1 - k) * flip(v, 1)

    ya, yb = p1(y), p2(y)
    yab = p2(ya)
    sib = at(x, zh, z, y, 1 - k)
    y_peers = [at(x, zh, z, lax.rem(y + d, NY), k) for d in range(1, NY)]
    z_peers = [at(x, zh, lax.rem(z + d, NZ), y, k) for d in range(1, NZ)]
    home = flip(z, 4)
    c_peers = [
        at(lax.rem(x + d, NX), lax.rem(zh + e, 2), home, y, k)
        for d in range(NX)
        for e in range(2)
    ]
    quad = [flip(z, 1), flip(z, 2), flip(flip(z, 1), 2)]

    def along_z(d):
        to = lax.rem(zh * NZ + z + d + 2 * NZ, 2 * NZ)
        return at(x, lax.div(to, NZ), lax.rem(to, NZ), y, k)

    z_near = [along_z(d) for d in (-2, 2, -1, 1)]
    x_peers = [at(lax.rem(x + d, NX), zh, z, y, k) for d in (2, 1, 3)]
    near = z_near + x_peers + y_peers + [sib]

    def tell(sem, devices):
        for p in devices:
            pl.semaphore_signal(sem, inc=1, device_id=p, device_id_type=MESH)

    loads = {}

    def load(name, src, dst):
        cp = pltpu.make_async_copy(src, dst, ins.at[len(loads)])
        cp.start()
        loads[name] = cp

    load("qa", qa, xqa)
    load("qg", qg, xqg)
    load("pa", pa, wa)
    load("pg", pg, wg)
    barrier = pltpu.get_barrier_semaphore()
    tell(barrier, near)
    zp = lax.div(z, 2)
    for w in range(NP - 1, -1, -1):
        b = flip(zp, 2)
        for bit in (1, 2):
            b = flip(b, bit) if w & bit else b
        cols = pl.ds(pl.multiple_of(b * (2 * BLOCK), 2 * BLOCK), 2 * BLOCK)
        load(f"ta{w}", ta.at[:, cols], xa.at[w])
        load(f"tg{w}", tg.at[cols], xg.at[w])
    load("seg", seg, xseg)
    load("lr", lr, xlr)

    sends, arrivals = {}, {}

    def copy(src, dst, to, out_of, into):
        return pltpu.make_async_remote_copy(
            src_ref=src, dst_ref=dst,
            send_sem=ssem.at[sends.setdefault(out_of, len(sends))],
            recv_sem=rsem.at[arrivals.setdefault(into, len(arrivals))],
            device_id=to, device_id_type=MESH,
        )

    def send(src, dst, to, out_of, into=None):
        copy(src, dst, to, out_of, into or out_of).start()

    def arrived(ref, into):
        copy(ref, ref, sib, "c", into).wait_recv()

    def left(ref, out_of):
        copy(ref, ref, sib, out_of, "qc").wait_send()

    def project(acts, grads, store):
        a = jnp.dot(wa[...], acts, preferred_element_type=jnp.float32)
        g = lax.dot_general(
            wg[...], grads, (((1,), (1,)), ((), ())), preferred_element_type=jnp.float32
        )
        for j in range(a.shape[1] // LANES):
            store(0, j, a[:, j * LANES : (j + 1) * LANES])
            store(1, j, g[:, j * LANES : (j + 1) * LANES])

    def project_query():
        for n in ("pa", "pg", "qa", "qg"):
            loads[n].wait()

        def store(h, j, v):
            qpart[h, j] = v

        project(xqa[...], xqg[...], store)

    def project_pair(w):
        loads[f"ta{w}"].wait()
        loads[f"tg{w}"].wait()

        def store(h, j, v):
            part[w, h, j // NY, j % NY] = v

        project(xa[w], xg[w], store)

    def send_c(w):
        send(part.at[w, 1 - k], c_in.at[w], sib, "c", ("c", w))

    def own(w, i, v):
        return part[w, k, i, v] + c_in[w, i, v]

    def stage_y1(w):
        arrived(c_in.at[w], ("c", w))
        put(y1_out.at[w], [[own(w, i, ya), own(w, i, yab)] for i in range(2)])
        send(y1_out.at[w], y1_in.at[w], at(x, zh, z, ya, k), "y1", ("y1", w))

    def stage_y2(w):
        arrived(y1_in.at[w], ("y1", w))
        got = get(y1_in.at[w], 2, HALF)
        put(y2_out.at[w], [[own(w, i, yb) + got[i][1]] for i in range(2)])
        send(y2_out.at[w], y2_in.at[w], at(x, zh, z, yb, k), "y2", ("y2", w))
        for i in range(2):
            keep[w, i] = own(w, i, y) + got[i][0]

    def stage_z(w):
        arrived(y2_in.at[w], ("y2", w))
        got = get(y2_in.at[w], 2, HALF)
        for i in range(2):
            keep[w, i] = keep[w, i] + got[i][0]
        far = w // 2
        for i, q in ((1, 2), (0, 1)) if w % 2 else ((1, 0),):
            put(z_out.at[far, q], [[keep[w, lax.rem(z + i, 2)]]])
            send(
                z_out.at[far, q], z_in.at[far, q], at(x, zh, quad[q], y, k), "z", ("z", far)
            )

    def quad_sum(far):
        arrived(z_in.at[far], ("z", far))
        v = keep[2 * far, lax.rem(z, 2)]
        for q in range(3):
            v = v + get(z_in.at[far, q], 1, HALF)[0][0]
        return v

    def stage_far():
        put(f_out, [[quad_sum(1)]])
        send(f_out, f_in, at(x, zh, home, y, k), "far")

    def stage_near():
        keep[0, 0] = quad_sum(0)

    project_query()
    project_pair(3)
    pl.semaphore_wait(barrier, len(near))
    send(qpart.at[1 - k], qc_in, sib, "qc")
    send_c(3)
    tell(z_sem, z_near)
    project_pair(2)
    send_c(2)
    arrived(qc_in, "qc")
    for j in range(NY):
        v = qpart[k, j] + qc_in[j]
        qy_own[j] = v
        put(qy_out.at[j], [[v]])
    for d in (2, 1, 3):
        send(qy_out.at[lax.rem(y + d, NY)], qy_in.at[d - 1], y_peers[d - 1], "qy")
    stage_y1(3)
    project_pair(1)
    send_c(1)
    stage_y1(2)
    project_pair(0)
    send_c(0)
    stage_y1(1)
    stage_y1(0)
    arrived(qy_in, "qy")
    v = qy_own[y]
    for d in range(NY - 1):
        v = v + get(qy_in.at[d], 1, HALF)[0][0]
    pl.semaphore_wait(z_sem, len(z_near))
    tell(x_sem, x_peers)
    middle = (NZ // 2 - 1, NZ // 2)
    for h in range(2):
        qz_own[h] = v[h * QH : (h + 1) * QH]
        put(qz_out.at[h], [[v[h * QH : (h + 1) * QH]]])

    def to_middle(h):
        d = lax.rem(z - middle[h] + NZ, NZ)
        return copy(
            qz_out.at[h], qz_in.at[d], at(x, zh, middle[h], y, k), ("mid", h), "mid"
        )

    for h in range(2):

        @pl.when(z != middle[h])
        def _():
            to_middle(h).start()

    is_middle = jnp.logical_or(z == middle[0], z == middle[1])
    my_h = 1 - lax.rem(z, 2)
    arrivals["all", 0] = len(arrivals)
    arrivals["all", 1] = len(arrivals)

    def from_middle(d):
        place = qall.at[y, my_h]
        return pltpu.make_async_remote_copy(
            src_ref=place, dst_ref=place, send_sem=ssem.at[sends.setdefault("all", len(sends))],
            recv_sem=rsem.at[arrivals["all", 0] + my_h], device_id=z_peers[d - 1],
            device_id_type=MESH,
        )

    def middle_sum():
        @pl.when(is_middle)
        def _():
            arrived(qz_in.at[1:], "mid")
            total = qz_own[my_h]
            for d in range(1, NZ):
                total = total + get(qz_in.at[d], 1, QH)[0][0]
            put(qall.at[y, my_h], [[total]])
            for d in range(1, NZ):
                from_middle(d).start()

    def middle_in():
        for h in range(2):

            @pl.when(z != middle[h])
            def _():
                arrived(qall.at[y, h], ("all", h))

    stage_y2(3)
    stage_y2(2)
    stage_y2(1)
    stage_z(3)
    stage_y2(0)
    stage_z(2)
    middle_sum()
    stage_z(1)
    stage_z(0)
    stage_far()
    loads["seg"].wait()
    loads["lr"].wait()
    onehot = jnp.where(
        lax.broadcasted_iota(jnp.int32, (NQ, QTOK), 0) == xseg[...], 1.0, 0.0
    ).astype(jnp.bfloat16)
    middle_in()
    line = qall.at[y]
    for d in (2, 1, 3):
        send(line, line, y_peers[d - 1], "line")
    stage_near()
    arrived(f_in, "far")
    tok = (keep[0, 0] + get(f_in, 1, HALF)[0][0]).T
    arrived(qall.at[1:], "line")
    for j in range(NY):
        feats = jnp.concatenate([get(qall.at[j, h], 1, QH)[0][0] for h in range(2)], axis=0)
        match = jnp.dot(
            tok, feats, precision=lax.Precision.HIGHEST, preferred_element_type=jnp.float32
        )
        p_out[:, j] = match.reshape(2, ROWS, LANES)
    send(p_out.at[1 - k], p_in, sib, "pc")
    arrived(p_in, "pc")
    score = jnp.zeros((NQ, LANES), jnp.float32)
    for j in range(NY):
        prod = p_out[k, j] * p_in[j]
        high = prod.astype(jnp.bfloat16)
        rest = (prod - high.astype(jnp.float32)).astype(jnp.bfloat16)
        score += lax.dot_general(
            onehot[:, j * LANES : (j + 1) * LANES],
            jnp.concatenate([high, rest], axis=0),
            (((1,), (1,)), ((), ())), preferred_element_type=jnp.float32,
        )
    score = (xlr[0] * (score + pltpu.roll(score, ROWS, 1))).reshape(8, 8, LANES)
    low = lax.broadcasted_iota(jnp.int32, s_out.shape, 2) < ROWS
    s_out[...] = jnp.where(low, score[:, :4], score[:, 4:])
    pl.semaphore_wait(x_sem, len(x_peers))
    for i, p in enumerate(c_peers):
        send(s_out.at[p[0]], s_in.at[i], p, "fin")
    arrived(s_in, "fin")
    total = s_in[0]
    for i in range(1, len(c_peers)):
        total = total + s_in[i]
    out[0:4] = total[:, :ROWS]
    out[4:8] = total[:, ROWS:]
    for ref, out_of in (
        (qc_in, "qc"), (c_in, "c"), (qy_in, "qy"), (y1_in, "y1"), (y2_in, "y2"), (z_in, "z"),
        (f_in, "far"), (qall.at[1:], "line"), (p_in, "pc"), (s_in, "fin"),
    ):
        left(ref, out_of)
    for h in range(2):

        @pl.when(z != middle[h])
        def _():
            left(qz_out.at[h], ("mid", h))

    @pl.when(is_middle)
    def _():
        left(qz_in.at[1:], "all")


def body(
    train_acts, train_grads, query_acts, query_grads, query_segment, proj_act, proj_grad, lrates
):
    ff, d = train_acts.shape[2], train_grads.shape[2]
    f32, bf16, i32 = jnp.float32, jnp.bfloat16, jnp.int32
    vmem = pltpu.VMEM
    hbm = pl.BlockSpec(memory_space=pltpu.HBM)
    res = pl.pallas_call(
        kernel,
        out_shape=jax.ShapeDtypeStruct((8, ROWS), f32),
        in_specs=[hbm] * 8,
        out_specs=pl.BlockSpec(memory_space=pltpu.VMEM),
        scratch_shapes=[
            vmem((NP, ff, 2 * BLOCK), bf16),
            vmem((NP, 2 * BLOCK, d), bf16),
            vmem((ff, QTOK), bf16),
            vmem((QTOK, d), bf16),
            vmem((1, QTOK), i32),
            vmem((HALF, ff), bf16),
            vmem((HALF, d), bf16),
            pltpu.SMEM((1,), f32),
            pltpu.SemaphoreType.DMA((2 * NP + 6,)),
            vmem((NP, 2, 2, NY, HALF, LANES), f32),
            vmem((NP, 2, NY, HALF, LANES), f32),
            vmem((NP, 2 * HALF + 2, LANES), i32),
            vmem((NP, 2 * HALF + 2, LANES), i32),
            vmem((NP, HALF + 2, LANES), i32),
            vmem((NP, HALF + 2, LANES), i32),
            vmem((2, 3, QH + 1, LANES), i32),
            vmem((2, 3, QH + 1, LANES), i32),
            vmem((QH + 1, LANES), i32),
            vmem((QH + 1, LANES), i32),
            vmem((NP, 2, HALF, LANES), f32),
            vmem((2, NY, HALF, LANES), f32),
            vmem((NY, HALF, LANES), f32),
            vmem((NY, HALF, LANES), f32),
            vmem((NY, QH + 1, LANES), i32),
            vmem((NY - 1, QH + 1, LANES), i32),
            vmem((2, QH, LANES), f32),
            vmem((2, QH // 2 + 1, LANES), i32),
            vmem((NZ, QH // 2 + 1, LANES), i32),
            vmem((NY, 2, QH // 2 + 1, LANES), i32),
            vmem((2, NY, ROWS, LANES), f32),
            vmem((NY, ROWS, LANES), f32),
            vmem((8, 4, LANES), f32),
            vmem((8, 4, LANES), f32),
            pltpu.SemaphoreType.DMA((13,)),
            pltpu.SemaphoreType.DMA((25,)),
            pltpu.SemaphoreType.REGULAR,
            pltpu.SemaphoreType.REGULAR,
        ],
        compiler_params=pltpu.CompilerParams(
            collective_id=0, has_side_effects=True, vmem_limit_bytes=60 << 20
        ),
        name="tracin",
    )(
        train_acts[0].T,
        train_grads[0],
        query_acts[0].T,
        query_grads[0],
        query_segment.reshape(1, QTOK),
        proj_act.T,
        proj_grad.T,
        lrates,
    )
    return res.T


def solution(mesh):
    placed = (
        P("ckpt", None, "unit"),
        P("ckpt", None, "unit"),
        P("ckpt", None, "unit"),
        P("ckpt", None, "unit"),
        P(),
        P("unit", None),
        P("unit", None),
        P("ckpt"),
    )
    return jax.shard_map(
        body, mesh=mesh, in_specs=placed, out_specs=P("unit", "ckpt"), check_vma=False
    )
```

```python
import jax
import jax.numpy as jnp
from jax import lax
from jax.experimental import pallas as pl
from jax.experimental.pallas import tpu as pltpu
from jax.sharding import PartitionSpec as P

MESH = pl.DeviceIdType.MESH
NX, NZ, NY = 4, 8, 4
NQ = 64
ROWS = 64
BLOCK = NY * 2 * ROWS
NP = NZ // 2
HALF = 64
QH = HALF // 2
QTOK = 512
LANES = 128
TOP = 32760.0


def flip(v, bit):
    return v + bit - 2 * bit * lax.rem(lax.div(v, bit), 2)


def put(ref, groups):
    at, logs = 0, []
    for blocks in groups:
        top = jnp.max(jnp.abs(blocks[0]), axis=0, keepdims=True)
        for v in blocks[1:]:
            top = jnp.maximum(top, jnp.max(jnp.abs(v), axis=0, keepdims=True))
        log = jnp.ceil(jnp.log2(jnp.maximum(top, 1e-30)) * 256.0)
        unit = jnp.exp2(log * (-1.0 / 256.0)) * TOP
        for v in blocks:
            q = jnp.round(v * unit).astype(jnp.int32)
            n = v.shape[0] // 2
            ref[at : at + n] = (q[n:] << 16) | (q[:n] & 0xFFFF)
            at += n
        logs.append(log.astype(jnp.int32))
    for log in logs:
        ref[at : at + 1] = log
        at += 1


def get(ref, groups, rows):
    n, half = ref.shape[0] - groups, rows // 2
    found = []
    for i in range(groups):
        log = ref[n + i : n + i + 1].astype(jnp.float32)
        unit = jnp.exp2(log * (1.0 / 256.0)) * (1.0 / TOP)
        blocks = []
        for r in range(i * n // groups, (i + 1) * n // groups, half):
            v = ref[r : r + half]
            both = jnp.concatenate([(v << 16) >> 16, v >> 16], axis=0)
            blocks.append(both.astype(jnp.float32) * unit)
        found.append(blocks)
    return found


def terms(v):
    high = v.astype(jnp.bfloat16).astype(jnp.float32)
    return high, (v - high).astype(jnp.bfloat16).astype(jnp.float32)


def kernel(
    ta, tg, qa, qg, seg, pa, pg, lr, out,
    xa, xg, xqa, xqg, xseg, wa, wg, ins,
    part, c_in, y1_out, y1_in, y2_out, y2_in, z_out, z_in, f_out, f_in, keep,
    qpart, qc_in, qy_own, qy_out, qy_in, qz_own, qz_out, qz_in, qall, p_out, p_in, s_out, s_in,
    ssem, rsem, z_sem, x_sem,
):
    c = lax.axis_index("ckpt")
    u = lax.axis_index("unit")
    x, zh = lax.div(c, 2), lax.rem(c, 2)
    z, y, k = lax.div(u, 8), lax.rem(lax.div(u, 2), 4), lax.rem(u, 2)

    def at(x_, zh_, z_, y_, k_):
        return (x_ * 2 + zh_, (z_ * NY + y_) * 2 + k_)

    def p1(v):
        return k * flip(v, 1) + (1 - k) * (3 - v)

    def p2(v):
        return k * (3 - v) + (1 - k) * flip(v, 1)

    ya, yb = p1(y), p2(y)
    yab = p2(ya)
    sib = at(x, zh, z, y, 1 - k)
    y_peers = [at(x, zh, z, lax.rem(y + d, NY), k) for d in range(1, NY)]
    z_peers = [at(x, zh, lax.rem(z + d, NZ), y, k) for d in range(1, NZ)]
    home = flip(z, 4)
    c_peers = [
        at(lax.rem(x + d, NX), lax.rem(zh + e, 2), home, y, k)
        for d in (0, 2, 1, 3)
        for e in range(2)
    ]
    quad = [flip(z, 1), flip(z, 2), flip(flip(z, 1), 2)]

    def along_z(d):
        to = lax.rem(zh * NZ + z + d + 2 * NZ, 2 * NZ)
        return at(x, lax.div(to, NZ), lax.rem(to, NZ), y, k)

    z_near = [along_z(d) for d in (-2, 2, -1, 1)]
    x_peers = [at(lax.rem(x + d, NX), zh, z, y, k) for d in (2, 1, 3)]
    near = z_near + x_peers + y_peers + [sib]

    def tell(sem, devices):
        for p in devices:
            pl.semaphore_signal(sem, inc=1, device_id=p, device_id_type=MESH)

    loads = {}

    def load(name, src, dst):
        cp = pltpu.make_async_copy(src, dst, ins.at[len(loads)])
        cp.start()
        loads[name] = cp

    load("qa", qa, xqa)
    load("qg", qg, xqg)
    load("pa", pa, wa)
    load("pg", pg, wg)
    barrier = pltpu.get_barrier_semaphore()
    tell(barrier, near)
    zp = lax.div(z, 2)
    for w in range(NP - 1, -1, -1):
        b = flip(zp, 2)
        for bit in (1, 2):
            b = flip(b, bit) if w & bit else b
        cols = pl.ds(pl.multiple_of(b * (2 * BLOCK), 2 * BLOCK), 2 * BLOCK)
        load(f"ta{w}", ta.at[:, cols], xa.at[w])
        load(f"tg{w}", tg.at[cols], xg.at[w])
    load("seg", seg, xseg)

    sends, arrivals = {}, {}

    def copy(src, dst, to, out_of, into):
        return pltpu.make_async_remote_copy(
            src_ref=src, dst_ref=dst,
            send_sem=ssem.at[sends.setdefault(out_of, len(sends))],
            recv_sem=rsem.at[arrivals.setdefault(into, len(arrivals))],
            device_id=to, device_id_type=MESH,
        )

    def send(src, dst, to, out_of, into=None):
        copy(src, dst, to, out_of, into or out_of).start()

    def arrived(ref, into):
        copy(ref, ref, sib, "c", into).wait_recv()

    def left(ref, out_of):
        copy(ref, ref, sib, out_of, "qc").wait_send()

    def project(acts, grads, store):
        a = jnp.dot(wa[...], acts, preferred_element_type=jnp.float32)
        g = lax.dot_general(
            wg[...], grads, (((1,), (1,)), ((), ())), preferred_element_type=jnp.float32
        )
        for j in range(a.shape[1] // LANES):
            store(0, j, a[:, j * LANES : (j + 1) * LANES])
            store(1, j, g[:, j * LANES : (j + 1) * LANES])

    def project_query():
        for n in ("pa", "pg", "qa", "qg"):
            loads[n].wait()

        def store(h, j, v):
            qpart[h, j] = v

        project(xqa[...], xqg[...], store)

    def project_pair(w):
        loads[f"ta{w}"].wait()
        loads[f"tg{w}"].wait()

        def store(h, j, v):
            part[w, h, j // NY, j % NY] = v

        project(xa[w], xg[w], store)

    def send_c(w):
        send(part.at[w, 1 - k], c_in.at[w], sib, "c", ("c", w))

    def own(w, i, v):
        return part[w, k, i, v] + c_in[w, i, v]

    def stage_y1(w):
        arrived(c_in.at[w], ("c", w))
        put(y1_out.at[w], [[own(w, i, ya), own(w, i, yab)] for i in range(2)])
        send(y1_out.at[w], y1_in.at[w], at(x, zh, z, ya, k), "y1", ("y1", w))

    def stage_y2(w):
        arrived(y1_in.at[w], ("y1", w))
        got = get(y1_in.at[w], 2, HALF)
        put(y2_out.at[w], [[own(w, i, yb) + got[i][1]] for i in range(2)])
        send(y2_out.at[w], y2_in.at[w], at(x, zh, z, yb, k), "y2", ("y2", w))
        for i in range(2):
            keep[w, i] = own(w, i, y) + got[i][0]

    def stage_z(w):
        arrived(y2_in.at[w], ("y2", w))
        got = get(y2_in.at[w], 2, HALF)
        for i in range(2):
            keep[w, i] = keep[w, i] + got[i][0]
        far = w // 2
        for i, q in ((1, 2), (0, 1)) if w % 2 else ((1, 0),):
            put(z_out.at[far, q], [[keep[w, lax.rem(z + i, 2)]]])
            send(
                z_out.at[far, q], z_in.at[far, q], at(x, zh, quad[q], y, k), "z", ("z", far)
            )

    def quad_sum(far):
        arrived(z_in.at[far], ("z", far))
        v = keep[2 * far, lax.rem(z, 2)]
        for q in range(3):
            v = v + get(z_in.at[far, q], 1, HALF)[0][0]
        return v

    def stage_far():
        put(f_out, [[quad_sum(1)]])
        send(f_out, f_in, at(x, zh, home, y, k), "far")

    def stage_near():
        keep[0, 0] = quad_sum(0)

    project_query()
    project_pair(3)
    pl.semaphore_wait(barrier, len(near))
    send(qpart.at[1 - k], qc_in, sib, "qc")
    send_c(3)
    tell(z_sem, z_near)
    project_pair(2)
    send_c(2)
    arrived(qc_in, "qc")
    for j in range(NY):
        v = qpart[k, j] + qc_in[j]
        qy_own[j] = v
        put(qy_out.at[j], [[v]])
    for d in (2, 1, 3):
        send(qy_out.at[lax.rem(y + d, NY)], qy_in.at[d - 1], y_peers[d - 1], "qy")
    stage_y1(3)
    project_pair(1)
    send_c(1)
    stage_y1(2)
    project_pair(0)
    send_c(0)
    stage_y1(1)
    stage_y1(0)
    arrived(qy_in, "qy")
    v = qy_own[y]
    for d in range(NY - 1):
        v = v + get(qy_in.at[d], 1, HALF)[0][0]
    pl.semaphore_wait(z_sem, len(z_near))
    tell(x_sem, x_peers)
    middle = (NZ // 2 - 1, NZ // 2)
    for h in range(2):
        qz_own[h] = v[h * QH : (h + 1) * QH]
        put(qz_out.at[h], [[v[h * QH : (h + 1) * QH]]])

    def to_middle(h):
        d = lax.rem(z - middle[h] + NZ, NZ)
        return copy(
            qz_out.at[h], qz_in.at[d], at(x, zh, middle[h], y, k), ("mid", h), "mid"
        )

    for h in range(2):

        @pl.when(z != middle[h])
        def _():
            to_middle(h).start()

    is_middle = jnp.logical_or(z == middle[0], z == middle[1])
    my_h = 1 - lax.rem(z, 2)
    arrivals["all", 0] = len(arrivals)
    arrivals["all", 1] = len(arrivals)

    def from_middle(d):
        place = qall.at[y, my_h]
        return pltpu.make_async_remote_copy(
            src_ref=place, dst_ref=place, send_sem=ssem.at[sends.setdefault("all", len(sends))],
            recv_sem=rsem.at[arrivals["all", 0] + my_h], device_id=z_peers[d - 1],
            device_id_type=MESH,
        )

    def middle_sum():
        @pl.when(is_middle)
        def _():
            arrived(qz_in.at[1:], "mid")
            total = qz_own[my_h]
            for d in range(1, NZ):
                total = total + get(qz_in.at[d], 1, QH)[0][0]
            put(qall.at[y, my_h], [[total]])
            for d in range(1, NZ):
                from_middle(d).start()

    def middle_in(h):
        @pl.when(z != middle[0] + h)
        def _():
            pltpu.make_async_remote_copy(
                src_ref=qall.at[y, h], dst_ref=qall.at[y, h], send_sem=ssem.at[0],
                recv_sem=rsem.at[arrivals["all", 0] + h], device_id=sib, device_id_type=MESH,
            ).wait_recv()

        for d in (2, 1, 3):
            send(qall.at[y, h], qall.at[y, h], y_peers[d - 1], "line")

    stage_y2(3)
    stage_y2(2)
    stage_y2(1)
    stage_z(3)
    stage_y2(0)
    stage_z(2)
    middle_sum()
    stage_far()
    stage_z(1)
    stage_z(0)
    loads["seg"].wait()
    onehot = jnp.where(
        lax.broadcasted_iota(jnp.int32, (NQ, QTOK), 0) == xseg[...], 1.0, 0.0
    ).astype(jnp.bfloat16)
    first_h = lax.div(z, NZ // 2)
    middle_in(first_h)
    middle_in(1 - first_h)
    stage_near()
    arrived(f_in, "far")
    tok = keep[0, 0] + get(f_in, 1, HALF)[0][0]
    high, rest = terms(tok)
    lhs = jnp.concatenate([high, high, rest], axis=0).T.astype(jnp.bfloat16)
    arrived(qall.at[1:], "line")
    rhs = []
    for j in range(NY):
        feats = jnp.concatenate([get(qall.at[j, h], 1, QH)[0][0] for h in range(2)], axis=0)
        high, rest = terms(feats)
        rhs.append(jnp.concatenate([high, rest, high], axis=0).astype(jnp.bfloat16))
    match = jnp.dot(lhs, jnp.concatenate(rhs, axis=1), preferred_element_type=jnp.float32)
    for j in range(NY):
        p_out[:, j] = match[:, j * LANES : (j + 1) * LANES].reshape(2, ROWS, LANES)
    send(p_out.at[1 - k], p_in, sib, "pc")
    arrived(p_in, "pc")
    score = jnp.zeros((NQ, LANES), jnp.float32)
    for j in range(NY):
        prod = p_out[k, j] * p_in[j]
        high, rest = terms(prod)
        score += lax.dot_general(
            onehot[:, j * LANES : (j + 1) * LANES],
            jnp.concatenate([high, rest], axis=0).astype(jnp.bfloat16),
            (((1,), (1,)), ((), ())), preferred_element_type=jnp.float32,
        )
    score = (lr[0] * (score + pltpu.roll(score, ROWS, 1))).reshape(8, 8, LANES)
    low = lax.broadcasted_iota(jnp.int32, s_out.shape, 2) < ROWS
    s_out[...] = jnp.where(low, score[:, :4], score[:, 4:])
    pl.semaphore_wait(x_sem, len(x_peers))
    for i, p in list(enumerate(c_peers))[2:] + list(enumerate(c_peers))[:2]:
        send(s_out.at[p[0]], s_in.at[i], p, "fin")
    arrived(s_in, "fin")
    total = s_in[0]
    for i in range(1, len(c_peers)):
        total = total + s_in[i]
    out[0:4] = total[:, :ROWS]
    out[4:8] = total[:, ROWS:]
    for ref, out_of in (
        (qc_in, "qc"), (c_in, "c"), (qy_in, "qy"), (y1_in, "y1"), (y2_in, "y2"), (z_in, "z"),
        (f_in, "far"), (qall.at[1:], "line"), (p_in, "pc"), (s_in, "fin"),
    ):
        left(ref, out_of)
    for h in range(2):

        @pl.when(z != middle[h])
        def _():
            left(qz_out.at[h], ("mid", h))

    @pl.when(is_middle)
    def _():
        left(qz_in.at[1:], "all")


def body(
    train_acts, train_grads, query_acts, query_grads, query_segment, proj_act, proj_grad, lrates
):
    ff, d = train_acts.shape[2], train_grads.shape[2]
    f32, bf16, i32 = jnp.float32, jnp.bfloat16, jnp.int32
    vmem = pltpu.VMEM
    hbm = pl.BlockSpec(memory_space=pltpu.HBM)
    res = pl.pallas_call(
        kernel,
        out_shape=pltpu.VMEM((8, ROWS), f32),
        in_specs=[hbm] * 7 + [pl.BlockSpec(memory_space=pltpu.SMEM)],
        out_specs=pl.BlockSpec(memory_space=pltpu.VMEM),
        scratch_shapes=[
            vmem((NP, ff, 2 * BLOCK), bf16),
            vmem((NP, 2 * BLOCK, d), bf16),
            vmem((ff, QTOK), bf16),
            vmem((QTOK, d), bf16),
            vmem((1, QTOK), i32),
            vmem((HALF, ff), bf16),
            vmem((HALF, d), bf16),
            pltpu.SemaphoreType.DMA((2 * NP + 5,)),
            vmem((NP, 2, 2, NY, HALF, LANES), f32),
            vmem((NP, 2, NY, HALF, LANES), f32),
            vmem((NP, 2 * HALF + 2, LANES), i32),
            vmem((NP, 2 * HALF + 2, LANES), i32),
            vmem((NP, HALF + 2, LANES), i32),
            vmem((NP, HALF + 2, LANES), i32),
            vmem((2, 3, QH + 1, LANES), i32),
            vmem((2, 3, QH + 1, LANES), i32),
            vmem((QH + 1, LANES), i32),
            vmem((QH + 1, LANES), i32),
            vmem((NP, 2, HALF, LANES), f32),
            vmem((2, NY, HALF, LANES), f32),
            vmem((NY, HALF, LANES), f32),
            vmem((NY, HALF, LANES), f32),
            vmem((NY, QH + 1, LANES), i32),
            vmem((NY - 1, QH + 1, LANES), i32),
            vmem((2, QH, LANES), f32),
            vmem((2, QH // 2 + 1, LANES), i32),
            vmem((NZ, QH // 2 + 1, LANES), i32),
            vmem((NY, 2, QH // 2 + 1, LANES), i32),
            vmem((2, NY, ROWS, LANES), f32),
            vmem((NY, ROWS, LANES), f32),
            vmem((8, 4, LANES), f32),
            vmem((8, 4, LANES), f32),
            pltpu.SemaphoreType.DMA((13,)),
            pltpu.SemaphoreType.DMA((25,)),
            pltpu.SemaphoreType.REGULAR,
            pltpu.SemaphoreType.REGULAR,
        ],
        compiler_params=pltpu.CompilerParams(
            collective_id=0, has_side_effects=True, vmem_limit_bytes=48 << 20
        ),
        name="tracin",
    )(
        *(
            pltpu.with_memory_space_constraint(v, pltpu.HBM)
            for v in (
                train_acts[0].T,
                train_grads[0],
                query_acts[0].T,
                query_grads[0],
                query_segment.reshape(1, QTOK),
                proj_act.T,
                proj_grad.T,
            )
        ),
        lrates,
    )
    return res.T


def solution(mesh):
    placed = (
        P("ckpt", None, "unit"),
        P("ckpt", None, "unit"),
        P("ckpt", None, "unit"),
        P("ckpt", None, "unit"),
        P(),
        P("unit", None),
        P("unit", None),
        P("ckpt"),
    )
    return jax.shard_map(
        body, mesh=mesh, in_specs=placed, out_specs=P("unit", "ckpt"), check_vma=False
    )
```

```python
import jax
import jax.numpy as jnp
from jax import lax
from jax.experimental import pallas as pl
from jax.experimental.pallas import tpu as pltpu
from jax.sharding import PartitionSpec as P

MESH = pl.DeviceIdType.MESH
NX, NZ, NY = 4, 8, 4
NQ = 64
ROWS = 64
BLOCK = NY * 2 * ROWS
NP = NZ // 2
HALF = 64
QH = HALF // 2
QTOK = 512
LANES = 128
TOP = 32760.0


def flip(v, bit):
    return v + bit - 2 * bit * lax.rem(lax.div(v, bit), 2)


def put(ref, groups):
    at, logs = 0, []
    for blocks in groups:
        top = jnp.max(jnp.abs(blocks[0]), axis=0, keepdims=True)
        for v in blocks[1:]:
            top = jnp.maximum(top, jnp.max(jnp.abs(v), axis=0, keepdims=True))
        log = jnp.ceil(jnp.log2(jnp.maximum(top, 1e-30)) * 256.0)
        unit = jnp.exp2(log * (-1.0 / 256.0)) * TOP
        for v in blocks:
            q = jnp.round(v * unit).astype(jnp.int32)
            n = v.shape[0] // 2
            ref[at : at + n] = (q[n:] << 16) | (q[:n] & 0xFFFF)
            at += n
        logs.append(log.astype(jnp.int32))
    for log in logs:
        ref[at : at + 1] = log
        at += 1


def get(ref, groups, rows):
    n, half = ref.shape[0] - groups, rows // 2
    found = []
    for i in range(groups):
        log = ref[n + i : n + i + 1].astype(jnp.float32)
        unit = jnp.exp2(log * (1.0 / 256.0)) * (1.0 / TOP)
        blocks = []
        for r in range(i * n // groups, (i + 1) * n // groups, half):
            v = ref[r : r + half]
            both = jnp.concatenate([(v << 16) >> 16, v >> 16], axis=0)
            blocks.append(both.astype(jnp.float32) * unit)
        found.append(blocks)
    return found


def terms(v):
    high = v.astype(jnp.bfloat16).astype(jnp.float32)
    return high, (v - high).astype(jnp.bfloat16).astype(jnp.float32)


def kernel(
    ta, tg, qa, qg, seg, pa, pg, lr, out,
    xa, xg, xqa, xqg, xseg, wa, wg, ins,
    part, c_in, y1_out, y1_in, y2_out, y2_in, z_out, z_in, f_out, f_in, keep,
    qpart, qc_in, qy_own, qy_out, qy_in, qz_own, qz_out, qz_in, qall, p_out, p_in, s_out, s_in,
    ssem, rsem, z_sem, x_sem,
):
    c = lax.axis_index("ckpt")
    u = lax.axis_index("unit")
    x, zh = lax.div(c, 2), lax.rem(c, 2)
    z, y, k = lax.div(u, 8), lax.rem(lax.div(u, 2), 4), lax.rem(u, 2)

    def at(x_, zh_, z_, y_, k_):
        return (x_ * 2 + zh_, (z_ * NY + y_) * 2 + k_)

    def p1(v):
        return k * flip(v, 1) + (1 - k) * (3 - v)

    def p2(v):
        return k * (3 - v) + (1 - k) * flip(v, 1)

    ya, yb = p1(y), p2(y)
    yab = p2(ya)
    sib = at(x, zh, z, y, 1 - k)
    y_peers = [at(x, zh, z, lax.rem(y + d, NY), k) for d in range(1, NY)]
    z_peers = [at(x, zh, lax.rem(z + d, NZ), y, k) for d in range(1, NZ)]
    home = flip(z, 4)
    c_peers = [
        at(lax.rem(x + d, NX), lax.rem(zh + e, 2), home, y, k)
        for d in (0, 2, 1, 3)
        for e in range(2)
    ]
    quad = [flip(z, 1), flip(z, 2), flip(flip(z, 1), 2)]

    def along_z(d):
        to = lax.rem(zh * NZ + z + d + 2 * NZ, 2 * NZ)
        return at(x, lax.div(to, NZ), lax.rem(to, NZ), y, k)

    z_near = [along_z(d) for d in (-2, 2, -1, 1)]
    x_peers = [at(lax.rem(x + d, NX), zh, z, y, k) for d in (2, 1, 3)]
    near = z_near + x_peers + y_peers + [sib]

    def tell(sem, devices):
        for p in devices:
            pl.semaphore_signal(sem, inc=1, device_id=p, device_id_type=MESH)

    loads = {}

    def load(name, src, dst):
        cp = pltpu.make_async_copy(src, dst, ins.at[len(loads)])
        cp.start()
        loads[name] = cp

    load("qa", qa, xqa)
    load("qg", qg, xqg)
    load("pa", pa, wa)
    load("pg", pg, wg)
    barrier = pltpu.get_barrier_semaphore()
    tell(barrier, near)
    zp = lax.div(z, 2)

    def load_pair(w):
        b = flip(zp, 2)
        for bit in (1, 2):
            b = flip(b, bit) if w & bit else b
        cols = pl.ds(pl.multiple_of(b * (2 * BLOCK), 2 * BLOCK), 2 * BLOCK)
        load(f"ta{w}", ta.at[:, cols], xa.at[w])
        load(f"tg{w}", tg.at[cols], xg.at[w])

    load_pair(3)

    sends, arrivals = {}, {}

    def copy(src, dst, to, out_of, into):
        return pltpu.make_async_remote_copy(
            src_ref=src, dst_ref=dst,
            send_sem=ssem.at[sends.setdefault(out_of, len(sends))],
            recv_sem=rsem.at[arrivals.setdefault(into, len(arrivals))],
            device_id=to, device_id_type=MESH,
        )

    def send(src, dst, to, out_of, into=None):
        copy(src, dst, to, out_of, into or out_of).start()

    def arrived(ref, into):
        copy(ref, ref, sib, "c", into).wait_recv()

    def left(ref, out_of):
        copy(ref, ref, sib, out_of, "qc").wait_send()

    def project(acts, grads, store):
        a = jnp.dot(wa[...], acts, preferred_element_type=jnp.float32)
        g = lax.dot_general(
            wg[...], grads, (((1,), (1,)), ((), ())), preferred_element_type=jnp.float32
        )
        for j in range(a.shape[1] // LANES):
            store(0, j, a[:, j * LANES : (j + 1) * LANES])
            store(1, j, g[:, j * LANES : (j + 1) * LANES])

    def project_query(then):
        for n in ("pa", "pg", "qa", "qg"):
            loads[n].wait()
        then()

        def store(h, j, v):
            qpart[h, j] = v

        project(xqa[...], xqg[...], store)

    def project_pair(w):
        loads[f"ta{w}"].wait()
        loads[f"tg{w}"].wait()

        def store(h, j, v):
            part[w, h, j // NY, j % NY] = v

        project(xa[w], xg[w], store)

    def send_c(w):
        send(part.at[w, 1 - k], c_in.at[w], sib, "c", ("c", w))

    def own(w, i, v):
        return part[w, k, i, v] + c_in[w, i, v]

    def stage_y1(w):
        arrived(c_in.at[w], ("c", w))
        put(y1_out.at[w], [[own(w, i, ya), own(w, i, yab)] for i in range(2)])
        send(y1_out.at[w], y1_in.at[w], at(x, zh, z, ya, k), "y1", ("y1", w))

    def stage_y2(w):
        arrived(y1_in.at[w], ("y1", w))
        got = get(y1_in.at[w], 2, HALF)
        put(y2_out.at[w], [[own(w, i, yb) + got[i][1]] for i in range(2)])
        send(y2_out.at[w], y2_in.at[w], at(x, zh, z, yb, k), "y2", ("y2", w))
        for i in range(2):
            keep[w, i] = own(w, i, y) + got[i][0]

    def stage_z(w):
        arrived(y2_in.at[w], ("y2", w))
        got = get(y2_in.at[w], 2, HALF)
        for i in range(2):
            keep[w, i] = keep[w, i] + got[i][0]
        far = w // 2
        for i, q in ((1, 2), (0, 1)) if w % 2 else ((1, 0),):
            put(z_out.at[far, q], [[keep[w, lax.rem(z + i, 2)]]])
            send(
                z_out.at[far, q], z_in.at[far, q], at(x, zh, quad[q], y, k), "z", ("z", far)
            )

    def quad_sum(far):
        arrived(z_in.at[far], ("z", far))
        v = keep[2 * far, lax.rem(z, 2)]
        for q in range(3):
            v = v + get(z_in.at[far, q], 1, HALF)[0][0]
        return v

    def stage_far():
        put(f_out, [[quad_sum(1)]])
        send(f_out, f_in, at(x, zh, home, y, k), "far")

    def stage_near():
        keep[0, 0] = quad_sum(0)

    project_query(lambda: [load_pair(w) for w in (2, 1, 0)] + [load("seg", seg, xseg)])
    pl.semaphore_wait(barrier, len(near))
    send(qpart.at[1 - k], qc_in, sib, "qc")
    project_pair(3)
    send_c(3)
    tell(z_sem, z_near)

    @pl.when(k == 1)
    def _():
        project_pair(2)
        send_c(2)

    arrived(qc_in, "qc")
    for j in range(NY):
        v = qpart[k, j] + qc_in[j]
        qy_own[j] = v
        put(qy_out.at[j], [[v]])
    for d in (2, 1, 3):
        send(qy_out.at[lax.rem(y + d, NY)], qy_in.at[d - 1], y_peers[d - 1], "qy")

    @pl.when(k == 0)
    def _():
        project_pair(2)
        send_c(2)

    stage_y1(3)
    project_pair(1)
    send_c(1)
    stage_y1(2)
    project_pair(0)
    send_c(0)
    stage_y1(1)
    stage_y1(0)
    arrived(qy_in, "qy")
    v = qy_own[y]
    for d in range(NY - 1):
        v = v + get(qy_in.at[d], 1, HALF)[0][0]
    pl.semaphore_wait(z_sem, len(z_near))
    tell(x_sem, x_peers)
    middle = (NZ // 2 - 1, NZ // 2)
    for h in range(2):
        qz_own[h] = v[h * QH : (h + 1) * QH]
        put(qz_out.at[h], [[v[h * QH : (h + 1) * QH]]])

    def to_middle(h):
        d = lax.rem(z - middle[h] + NZ, NZ)
        return copy(
            qz_out.at[h], qz_in.at[d], at(x, zh, middle[h], y, k), ("mid", h), "mid"
        )

    for h in range(2):

        @pl.when(z != middle[h])
        def _():
            to_middle(h).start()

    is_middle = jnp.logical_or(z == middle[0], z == middle[1])
    my_h = 1 - lax.rem(z, 2)
    arrivals["all", 0] = len(arrivals)
    arrivals["all", 1] = len(arrivals)

    def from_middle(d):
        place = qall.at[y, my_h]
        return pltpu.make_async_remote_copy(
            src_ref=place, dst_ref=place, send_sem=ssem.at[sends.setdefault("all", len(sends))],
            recv_sem=rsem.at[arrivals["all", 0] + my_h], device_id=z_peers[d - 1],
            device_id_type=MESH,
        )

    def middle_sum():
        @pl.when(is_middle)
        def _():
            arrived(qz_in.at[1:], "mid")
            total = qz_own[my_h]
            for d in range(1, NZ):
                total = total + get(qz_in.at[d], 1, QH)[0][0]
            put(qall.at[y, my_h], [[total]])
            for d in range(1, NZ):
                from_middle(d).start()

    def middle_in(h):
        @pl.when(z != middle[0] + h)
        def _():
            pltpu.make_async_remote_copy(
                src_ref=qall.at[y, h], dst_ref=qall.at[y, h], send_sem=ssem.at[0],
                recv_sem=rsem.at[arrivals["all", 0] + h], device_id=sib, device_id_type=MESH,
            ).wait_recv()

        for d in (2, 1, 3):
            send(qall.at[y, h], qall.at[y, h], y_peers[d - 1], "line")

    stage_y2(3)
    stage_y2(2)
    stage_y2(1)
    stage_z(3)
    stage_y2(0)
    stage_z(2)
    middle_sum()
    stage_far()
    stage_z(1)
    stage_z(0)
    loads["seg"].wait()
    onehot = jnp.where(
        lax.broadcasted_iota(jnp.int32, (NQ, QTOK), 0) == xseg[...], 1.0, 0.0
    ).astype(jnp.bfloat16)
    first_h = lax.div(z, NZ // 2)
    middle_in(first_h)
    middle_in(1 - first_h)
    stage_near()
    arrived(f_in, "far")
    tok = keep[0, 0] + get(f_in, 1, HALF)[0][0]
    high, rest = terms(tok)
    lhs = jnp.concatenate([high, high, rest], axis=0).T.astype(jnp.bfloat16)
    arrived(qall.at[1:], "line")
    rhs = []
    for j in range(NY):
        feats = jnp.concatenate([get(qall.at[j, h], 1, QH)[0][0] for h in range(2)], axis=0)
        high, rest = terms(feats)
        rhs.append(jnp.concatenate([high, rest, high], axis=0).astype(jnp.bfloat16))
    match = jnp.dot(lhs, jnp.concatenate(rhs, axis=1), preferred_element_type=jnp.float32)
    for j in range(NY):
        p_out[:, j] = match[:, j * LANES : (j + 1) * LANES].reshape(2, ROWS, LANES)
    send(p_out.at[1 - k], p_in, sib, "pc")
    arrived(p_in, "pc")
    score = jnp.zeros((NQ, LANES), jnp.float32)
    for j in range(NY):
        prod = p_out[k, j] * p_in[j]
        high, rest = terms(prod)
        score += lax.dot_general(
            onehot[:, j * LANES : (j + 1) * LANES],
            jnp.concatenate([high, rest], axis=0).astype(jnp.bfloat16),
            (((1,), (1,)), ((), ())), preferred_element_type=jnp.float32,
        )
    score = (lr[0] * (score + pltpu.roll(score, ROWS, 1))).reshape(8, 8, LANES)
    low = lax.broadcasted_iota(jnp.int32, s_out.shape, 2) < ROWS
    s_out[...] = jnp.where(low, score[:, :4], score[:, 4:])
    pl.semaphore_wait(x_sem, len(x_peers))
    for i, p in list(enumerate(c_peers))[2:] + list(enumerate(c_peers))[:2]:
        send(s_out.at[p[0]], s_in.at[i], p, "fin")
    arrived(s_in, "fin")
    total = s_in[0]
    for i in range(1, len(c_peers)):
        total = total + s_in[i]
    out[0:4] = total[:, :ROWS]
    out[4:8] = total[:, ROWS:]
    for ref, out_of in (
        (qc_in, "qc"), (c_in, "c"), (qy_in, "qy"), (y1_in, "y1"), (y2_in, "y2"), (z_in, "z"),
        (f_in, "far"), (qall.at[1:], "line"), (p_in, "pc"), (s_in, "fin"),
    ):
        left(ref, out_of)
    for h in range(2):

        @pl.when(z != middle[h])
        def _():
            left(qz_out.at[h], ("mid", h))

    @pl.when(is_middle)
    def _():
        left(qz_in.at[1:], "all")


def body(
    train_acts, train_grads, query_acts, query_grads, query_segment, proj_act, proj_grad, lrates
):
    ff, d = train_acts.shape[2], train_grads.shape[2]
    f32, bf16, i32 = jnp.float32, jnp.bfloat16, jnp.int32
    vmem = pltpu.VMEM
    hbm = pl.BlockSpec(memory_space=pltpu.HBM)
    res = pl.pallas_call(
        kernel,
        out_shape=pltpu.VMEM((8, ROWS), f32),
        in_specs=[hbm] * 7 + [pl.BlockSpec(memory_space=pltpu.SMEM)],
        out_specs=pl.BlockSpec(memory_space=pltpu.VMEM),
        scratch_shapes=[
            vmem((NP, ff, 2 * BLOCK), bf16),
            vmem((NP, 2 * BLOCK, d), bf16),
            vmem((ff, QTOK), bf16),
            vmem((QTOK, d), bf16),
            vmem((1, QTOK), i32),
            vmem((HALF, ff), bf16),
            vmem((HALF, d), bf16),
            pltpu.SemaphoreType.DMA((2 * NP + 5,)),
            vmem((NP, 2, 2, NY, HALF, LANES), f32),
            vmem((NP, 2, NY, HALF, LANES), f32),
            vmem((NP, 2 * HALF + 2, LANES), i32),
            vmem((NP, 2 * HALF + 2, LANES), i32),
            vmem((NP, HALF + 2, LANES), i32),
            vmem((NP, HALF + 2, LANES), i32),
            vmem((2, 3, QH + 1, LANES), i32),
            vmem((2, 3, QH + 1, LANES), i32),
            vmem((QH + 1, LANES), i32),
            vmem((QH + 1, LANES), i32),
            vmem((NP, 2, HALF, LANES), f32),
            vmem((2, NY, HALF, LANES), f32),
            vmem((NY, HALF, LANES), f32),
            vmem((NY, HALF, LANES), f32),
            vmem((NY, QH + 1, LANES), i32),
            vmem((NY - 1, QH + 1, LANES), i32),
            vmem((2, QH, LANES), f32),
            vmem((2, QH // 2 + 1, LANES), i32),
            vmem((NZ, QH // 2 + 1, LANES), i32),
            vmem((NY, 2, QH // 2 + 1, LANES), i32),
            vmem((2, NY, ROWS, LANES), f32),
            vmem((NY, ROWS, LANES), f32),
            vmem((8, 4, LANES), f32),
            vmem((8, 4, LANES), f32),
            pltpu.SemaphoreType.DMA((13,)),
            pltpu.SemaphoreType.DMA((25,)),
            pltpu.SemaphoreType.REGULAR,
            pltpu.SemaphoreType.REGULAR,
        ],
        compiler_params=pltpu.CompilerParams(
            collective_id=0, has_side_effects=True, vmem_limit_bytes=48 << 20
        ),
        name="tracin",
    )(
        *(
            pltpu.with_memory_space_constraint(v, pltpu.HBM)
            for v in (
                train_acts[0].T,
                train_grads[0],
                query_acts[0].T,
                query_grads[0],
                query_segment.reshape(1, QTOK),
                proj_act.T,
                proj_grad.T,
            )
        ),
        lrates,
    )
    return res.T


def solution(mesh):
    placed = (
        P("ckpt", None, "unit"),
        P("ckpt", None, "unit"),
        P("ckpt", None, "unit"),
        P("ckpt", None, "unit"),
        P(),
        P("unit", None),
        P("unit", None),
        P("ckpt"),
    )
    return jax.shard_map(
        body, mesh=mesh, in_specs=placed, out_specs=P("unit", "ckpt"), check_vma=False
    )
```

```python
import jax
import jax.numpy as jnp
from jax import lax
from jax.experimental import pallas as pl
from jax.experimental.pallas import tpu as pltpu
from jax.sharding import PartitionSpec as P

MESH = pl.DeviceIdType.MESH
NX, NZ, NY = 4, 8, 4
NQ = 64
ROWS = 64
BLOCK = NY * 2 * ROWS
NP = NZ // 2
HALF = 64
QH = HALF // 2
QTOK = 512
LANES = 128
TOP = 32760.0


def flip(v, bit):
    return v + bit - 2 * bit * lax.rem(lax.div(v, bit), 2)


def put(ref, groups):
    at, logs = 0, []
    for blocks in groups:
        top = jnp.max(jnp.abs(blocks[0]), axis=0, keepdims=True)
        for v in blocks[1:]:
            top = jnp.maximum(top, jnp.max(jnp.abs(v), axis=0, keepdims=True))
        log = jnp.ceil(jnp.log2(jnp.maximum(top, 1e-30)) * 256.0)
        unit = jnp.exp2(log * (-1.0 / 256.0)) * TOP
        for v in blocks:
            q = jnp.round(v * unit).astype(jnp.int32)
            n = v.shape[0] // 2
            ref[at : at + n] = (q[n:] << 16) | (q[:n] & 0xFFFF)
            at += n
        logs.append(log.astype(jnp.int32))
    for log in logs:
        ref[at : at + 1] = log
        at += 1


def get(ref, groups, rows):
    n, half = ref.shape[0] - groups, rows // 2
    found = []
    for i in range(groups):
        log = ref[n + i : n + i + 1].astype(jnp.float32)
        unit = jnp.exp2(log * (1.0 / 256.0)) * (1.0 / TOP)
        blocks = []
        for r in range(i * n // groups, (i + 1) * n // groups, half):
            v = ref[r : r + half]
            both = jnp.concatenate([(v << 16) >> 16, v >> 16], axis=0)
            blocks.append(both.astype(jnp.float32) * unit)
        found.append(blocks)
    return found


def terms(v):
    high = v.astype(jnp.bfloat16).astype(jnp.float32)
    return high, (v - high).astype(jnp.bfloat16).astype(jnp.float32)


def kernel(
    ta, tg, qa, qg, seg, pa, pg, lr, out,
    xa, xg, xqa, xqg, xseg, wa, wg, ins,
    part, c_in, y1_out, y1_in, y2_out, y2_in, z_out, z_in, f_out, f_in, keep,
    qpart, qc_in, qy_own, qy_out, qy_in, qz_own, qz_out, qz_in, qall, p_out, p_in, s_out, s_in,
    ssem, rsem, z_sem, x_sem,
):
    c = lax.axis_index("ckpt")
    u = lax.axis_index("unit")
    x, zh = lax.div(c, 2), lax.rem(c, 2)
    z, y, k = lax.div(u, 8), lax.rem(lax.div(u, 2), 4), lax.rem(u, 2)

    def at(x_, zh_, z_, y_, k_):
        return (x_ * 2 + zh_, (z_ * NY + y_) * 2 + k_)

    def p1(v):
        return k * flip(v, 1) + (1 - k) * (3 - v)

    def p2(v):
        return k * (3 - v) + (1 - k) * flip(v, 1)

    ya, yb = p1(y), p2(y)
    yab = p2(ya)
    sib = at(x, zh, z, y, 1 - k)
    y_peers = [at(x, zh, z, lax.rem(y + d, NY), k) for d in range(1, NY)]
    z_peers = [at(x, zh, lax.rem(z + d, NZ), y, k) for d in range(1, NZ)]
    home = flip(z, 4)
    c_peers = [
        at(lax.rem(x + d, NX), lax.rem(zh + e, 2), home, y, k)
        for d in (0, 2, 1, 3)
        for e in range(2)
    ]
    quad = [flip(z, 1), flip(z, 2), flip(flip(z, 1), 2)]

    def along_z(d):
        to = lax.rem(zh * NZ + z + d + 2 * NZ, 2 * NZ)
        return at(x, lax.div(to, NZ), lax.rem(to, NZ), y, k)

    z_near = [along_z(d) for d in (-2, 2, -1, 1)]
    x_peers = [at(lax.rem(x + d, NX), zh, z, y, k) for d in (2, 1, 3)]
    near = z_near + x_peers + y_peers + [sib]

    def tell(sem, devices):
        for p in devices:
            pl.semaphore_signal(sem, inc=1, device_id=p, device_id_type=MESH)

    loads = {}

    def load(name, src, dst):
        cp = pltpu.make_async_copy(src, dst, ins.at[len(loads)])
        cp.start()
        loads[name] = cp

    load("qa", qa, xqa)
    load("qg", qg, xqg)
    load("pa", pa, wa)
    load("pg", pg, wg)
    barrier = pltpu.get_barrier_semaphore()
    tell(barrier, near)
    zp = lax.div(z, 2)

    def load_pair(w):
        b = flip(zp, 2)
        for bit in (1, 2):
            b = flip(b, bit) if w & bit else b
        cols = pl.ds(pl.multiple_of(b * (2 * BLOCK), 2 * BLOCK), 2 * BLOCK)
        load(f"ta{w}", ta.at[:, cols], xa.at[w])
        load(f"tg{w}", tg.at[cols], xg.at[w])

    load_pair(3)

    sends, arrivals = {}, {}

    def copy(src, dst, to, out_of, into):
        return pltpu.make_async_remote_copy(
            src_ref=src, dst_ref=dst,
            send_sem=ssem.at[sends.setdefault(out_of, len(sends))],
            recv_sem=rsem.at[arrivals.setdefault(into, len(arrivals))],
            device_id=to, device_id_type=MESH,
        )

    def send(src, dst, to, out_of, into=None):
        copy(src, dst, to, out_of, into or out_of).start()

    def arrived(ref, into):
        copy(ref, ref, sib, "c", into).wait_recv()

    def left(ref, out_of):
        copy(ref, ref, sib, out_of, "qc").wait_send()

    def project(acts, grads, store):
        a = jnp.dot(wa[...], acts, preferred_element_type=jnp.float32)
        g = lax.dot_general(
            wg[...], grads, (((1,), (1,)), ((), ())), preferred_element_type=jnp.float32
        )
        for j in range(a.shape[1] // LANES):
            store(0, j, a[:, j * LANES : (j + 1) * LANES])
            store(1, j, g[:, j * LANES : (j + 1) * LANES])

    def project_query(then):
        for n in ("pa", "pg", "qa", "qg"):
            loads[n].wait()
        then()

        def store(h, j, v):
            qpart[h, j] = v

        project(xqa[...], xqg[...], store)

    def project_pair(w):
        loads[f"ta{w}"].wait()
        loads[f"tg{w}"].wait()

        def store(h, j, v):
            part[w, h, j // NY, j % NY] = v

        project(xa[w], xg[w], store)

    def send_c(w):
        send(part.at[w, 1 - k], c_in.at[w], sib, "c", ("c", w))

    def own(w, i, v):
        return part[w, k, i, v] + c_in[w, i, v]

    def stage_y1(w):
        arrived(c_in.at[w], ("c", w))
        put(y1_out.at[w], [[own(w, i, ya), own(w, i, yab)] for i in range(2)])
        send(y1_out.at[w], y1_in.at[w], at(x, zh, z, ya, k), "y1", ("y1", w))

    def stage_y2(w):
        arrived(y1_in.at[w], ("y1", w))
        got = get(y1_in.at[w], 2, HALF)
        put(y2_out.at[w], [[own(w, i, yb) + got[i][1]] for i in range(2)])
        send(y2_out.at[w], y2_in.at[w], at(x, zh, z, yb, k), "y2", ("y2", w))
        for i in range(2):
            keep[w, i] = own(w, i, y) + got[i][0]

    def stage_z(w):
        arrived(y2_in.at[w], ("y2", w))
        got = get(y2_in.at[w], 2, HALF)
        for i in range(2):
            keep[w, i] = keep[w, i] + got[i][0]
        far = w // 2
        for i, q in ((1, 2), (0, 1)) if w % 2 else ((1, 0),):
            put(z_out.at[far, q], [[keep[w, lax.rem(z + i, 2)]]])
            send(
                z_out.at[far, q], z_in.at[far, q], at(x, zh, quad[q], y, k), "z", ("z", far)
            )

    def quad_sum(far):
        arrived(z_in.at[far], ("z", far))
        v = keep[2 * far, lax.rem(z, 2)]
        for q in range(3):
            v = v + get(z_in.at[far, q], 1, HALF)[0][0]
        return v

    def stage_far():
        put(f_out, [[quad_sum(1)]])
        send(f_out, f_in, at(x, zh, home, y, k), "far")

    def stage_near():
        keep[0, 0] = quad_sum(0)

    project_query(lambda: [load_pair(w) for w in (2, 1, 0)] + [load("seg", seg, xseg)])
    pl.semaphore_wait(barrier, len(near))
    send(qpart.at[1 - k], qc_in, sib, "qc")
    project_pair(3)
    send_c(3)
    tell(z_sem, z_near)

    @pl.when(k == 1)
    def _():
        for w in (2, 1):
            project_pair(w)
            send_c(w)

    arrived(qc_in, "qc")
    for j in range(NY):
        v = qpart[k, j] + qc_in[j]
        qy_own[j] = v
        put(qy_out.at[j], [[v]])
    for d in (2, 1, 3):
        send(qy_out.at[lax.rem(y + d, NY)], qy_in.at[d - 1], y_peers[d - 1], "qy")

    @pl.when(k == 0)
    def _():
        project_pair(2)
        send_c(2)

    stage_y1(3)

    @pl.when(k == 0)
    def _():
        project_pair(1)
        send_c(1)

    stage_y1(2)
    project_pair(0)
    send_c(0)
    stage_y1(1)
    stage_y1(0)
    arrived(qy_in, "qy")
    v = qy_own[y]
    for d in range(NY - 1):
        v = v + get(qy_in.at[d], 1, HALF)[0][0]
    pl.semaphore_wait(z_sem, len(z_near))
    tell(x_sem, x_peers)
    middle = (NZ // 2 - 1, NZ // 2)
    for h in range(2):
        qz_own[h] = v[h * QH : (h + 1) * QH]
        put(qz_out.at[h], [[v[h * QH : (h + 1) * QH]]])

    def to_middle(h):
        d = lax.rem(z - middle[h] + NZ, NZ)
        return copy(
            qz_out.at[h], qz_in.at[d], at(x, zh, middle[h], y, k), ("mid", h), "mid"
        )

    for h in range(2):

        @pl.when(z != middle[h])
        def _():
            to_middle(h).start()

    is_middle = jnp.logical_or(z == middle[0], z == middle[1])
    my_h = 1 - lax.rem(z, 2)
    arrivals["all", 0] = len(arrivals)
    arrivals["all", 1] = len(arrivals)

    def from_middle(d):
        place = qall.at[y, my_h]
        return pltpu.make_async_remote_copy(
            src_ref=place, dst_ref=place, send_sem=ssem.at[sends.setdefault("all", len(sends))],
            recv_sem=rsem.at[arrivals["all", 0] + my_h], device_id=z_peers[d - 1],
            device_id_type=MESH,
        )

    def middle_sum():
        @pl.when(is_middle)
        def _():
            arrived(qz_in.at[1:], "mid")
            total = qz_own[my_h]
            for d in range(1, NZ):
                total = total + get(qz_in.at[d], 1, QH)[0][0]
            put(qall.at[y, my_h], [[total]])
            for d in range(1, NZ):
                from_middle(d).start()

    def middle_in(h):
        @pl.when(z != middle[0] + h)
        def _():
            pltpu.make_async_remote_copy(
                src_ref=qall.at[y, h], dst_ref=qall.at[y, h], send_sem=ssem.at[0],
                recv_sem=rsem.at[arrivals["all", 0] + h], device_id=sib, device_id_type=MESH,
            ).wait_recv()

        for d in (2, 1, 3):
            send(qall.at[y, h], qall.at[y, h], y_peers[d - 1], "line")

    stage_y2(3)
    stage_y2(2)
    stage_y2(1)
    stage_z(3)
    stage_y2(0)
    stage_z(2)
    middle_sum()
    stage_far()
    stage_z(1)
    stage_z(0)
    loads["seg"].wait()
    onehot = jnp.where(
        lax.broadcasted_iota(jnp.int32, (NQ, QTOK), 0) == xseg[...], 1.0, 0.0
    ).astype(jnp.bfloat16)
    first_h = lax.div(z, NZ // 2)
    middle_in(first_h)
    middle_in(1 - first_h)
    stage_near()
    arrived(f_in, "far")
    tok = keep[0, 0] + get(f_in, 1, HALF)[0][0]
    high, rest = terms(tok)
    lhs = jnp.concatenate([high, high, rest], axis=0).T.astype(jnp.bfloat16)
    arrived(qall.at[1:], "line")
    rhs = []
    for j in range(NY):
        feats = jnp.concatenate([get(qall.at[j, h], 1, QH)[0][0] for h in range(2)], axis=0)
        high, rest = terms(feats)
        rhs.append(jnp.concatenate([high, rest, high], axis=0).astype(jnp.bfloat16))
    match = jnp.dot(lhs, jnp.concatenate(rhs, axis=1), preferred_element_type=jnp.float32)
    for j in range(NY):
        p_out[:, j] = match[:, j * LANES : (j + 1) * LANES].reshape(2, ROWS, LANES)
    send(p_out.at[1 - k], p_in, sib, "pc")
    arrived(p_in, "pc")
    score = jnp.zeros((NQ, LANES), jnp.float32)
    for j in range(NY):
        prod = p_out[k, j] * p_in[j]
        high, rest = terms(prod)
        score += lax.dot_general(
            onehot[:, j * LANES : (j + 1) * LANES],
            jnp.concatenate([high, rest], axis=0).astype(jnp.bfloat16),
            (((1,), (1,)), ((), ())), preferred_element_type=jnp.float32,
        )
    score = (lr[0] * (score + pltpu.roll(score, ROWS, 1))).reshape(8, 8, LANES)
    low = lax.broadcasted_iota(jnp.int32, s_out.shape, 2) < ROWS
    s_out[...] = jnp.where(low, score[:, :4], score[:, 4:])
    pl.semaphore_wait(x_sem, len(x_peers))
    for i, p in list(enumerate(c_peers))[2:] + list(enumerate(c_peers))[:2]:
        send(s_out.at[p[0]], s_in.at[i], p, "fin")
    arrived(s_in, "fin")
    total = s_in[0]
    for i in range(1, len(c_peers)):
        total = total + s_in[i]
    out[0:4] = total[:, :ROWS]
    out[4:8] = total[:, ROWS:]
    for ref, out_of in (
        (qc_in, "qc"), (c_in, "c"), (qy_in, "qy"), (y1_in, "y1"), (y2_in, "y2"), (z_in, "z"),
        (f_in, "far"), (qall.at[1:], "line"), (p_in, "pc"), (s_in, "fin"),
    ):
        left(ref, out_of)
    for h in range(2):

        @pl.when(z != middle[h])
        def _():
            left(qz_out.at[h], ("mid", h))

    @pl.when(is_middle)
    def _():
        left(qz_in.at[1:], "all")


def body(
    train_acts, train_grads, query_acts, query_grads, query_segment, proj_act, proj_grad, lrates
):
    ff, d = train_acts.shape[2], train_grads.shape[2]
    f32, bf16, i32 = jnp.float32, jnp.bfloat16, jnp.int32
    vmem = pltpu.VMEM
    hbm = pl.BlockSpec(memory_space=pltpu.HBM)
    res = pl.pallas_call(
        kernel,
        out_shape=pltpu.VMEM((8, ROWS), f32),
        in_specs=[hbm] * 7 + [pl.BlockSpec(memory_space=pltpu.SMEM)],
        out_specs=pl.BlockSpec(memory_space=pltpu.VMEM),
        scratch_shapes=[
            vmem((NP, ff, 2 * BLOCK), bf16),
            vmem((NP, 2 * BLOCK, d), bf16),
            vmem((ff, QTOK), bf16),
            vmem((QTOK, d), bf16),
            vmem((1, QTOK), i32),
            vmem((HALF, ff), bf16),
            vmem((HALF, d), bf16),
            pltpu.SemaphoreType.DMA((2 * NP + 5,)),
            vmem((NP, 2, 2, NY, HALF, LANES), f32),
            vmem((NP, 2, NY, HALF, LANES), f32),
            vmem((NP, 2 * HALF + 2, LANES), i32),
            vmem((NP, 2 * HALF + 2, LANES), i32),
            vmem((NP, HALF + 2, LANES), i32),
            vmem((NP, HALF + 2, LANES), i32),
            vmem((2, 3, QH + 1, LANES), i32),
            vmem((2, 3, QH + 1, LANES), i32),
            vmem((QH + 1, LANES), i32),
            vmem((QH + 1, LANES), i32),
            vmem((NP, 2, HALF, LANES), f32),
            vmem((2, NY, HALF, LANES), f32),
            vmem((NY, HALF, LANES), f32),
            vmem((NY, HALF, LANES), f32),
            vmem((NY, QH + 1, LANES), i32),
            vmem((NY - 1, QH + 1, LANES), i32),
            vmem((2, QH, LANES), f32),
            vmem((2, QH // 2 + 1, LANES), i32),
            vmem((NZ, QH // 2 + 1, LANES), i32),
            vmem((NY, 2, QH // 2 + 1, LANES), i32),
            vmem((2, NY, ROWS, LANES), f32),
            vmem((NY, ROWS, LANES), f32),
            vmem((8, 4, LANES), f32),
            vmem((8, 4, LANES), f32),
            pltpu.SemaphoreType.DMA((13,)),
            pltpu.SemaphoreType.DMA((25,)),
            pltpu.SemaphoreType.REGULAR,
            pltpu.SemaphoreType.REGULAR,
        ],
        compiler_params=pltpu.CompilerParams(
            collective_id=0, has_side_effects=True, vmem_limit_bytes=48 << 20
        ),
        name="tracin",
    )(
        *(
            pltpu.with_memory_space_constraint(v, pltpu.HBM)
            for v in (
                train_acts[0].T,
                train_grads[0],
                query_acts[0].T,
                query_grads[0],
                query_segment.reshape(1, QTOK),
                proj_act.T,
                proj_grad.T,
            )
        ),
        lrates,
    )
    return res.T


def solution(mesh):
    placed = (
        P("ckpt", None, "unit"),
        P("ckpt", None, "unit"),
        P("ckpt", None, "unit"),
        P("ckpt", None, "unit"),
        P(),
        P("unit", None),
        P("unit", None),
        P("ckpt"),
    )
    return jax.shard_map(
        body, mesh=mesh, in_specs=placed, out_specs=P("unit", "ckpt"), check_vma=False
    )
```
